512 devices in a mesh: dp: 16 (over y, x), expert: 32 (over z, core).
Axes of the slice: x: 4, y: 4, z: 16, core: 2. Of those that a mesh axis runs over, the one named last changes fastest.
Arguments:
- inputs: bfloat16 [2048, 6144], P('expert', 'dp'), may hold values from -6 to 6
- grad_out: bfloat16 [2048, 6144], P('expert', 'dp'), may hold values from -6 to 6
- expert_ids: int32 [2048, 2], P('expert'), may hold values from 0 to 3, as said below
- live_counts: int32 [32], P('expert'), may hold values from 32 to 64, as said below
- router_weight: bfloat16 [6144, 4], P('dp'), may hold values from -0.078125 to 0.078125
- up_weight: bfloat16 [6144, 32768], P('dp', 'expert'), may hold values from -0.078125 to 0.078125
- down_weight: bfloat16 [6144, 32768], P('dp', 'expert'), may hold values from -0.0625 to 0.0625
Outputs:
- grad_inputs: bfloat16 [2048, 6144], P('expert', 'dp')
- grad_up: bfloat16 [6144, 32768], P('dp', 'expert')
- grad_down: bfloat16 [6144, 32768], P('dp', 'expert')
- grad_router: float32 [6144, 4], P('dp')
The draws below stay inside these ranges and needn't reach their ends.
Inputs may be any that keep to these rules, and one draw needn't show every extreme that they name: `expert_ids`: each row names two different experts. Among the first live_counts[g] tokens of group g, each expert is named at most 32 times; one expert is named exactly 32 times in every group. `live_counts`: some group has all its slots live.
All inputs are finite; a program needn't handle non-finite values.
Results may differ from the reference program's by a relative error of at most 0.035.
Values may be sent and summed in bfloat16 or wider, within the bound.
A program may use at most 64 MiB of HBM per device.

```python
import jax
import jax.numpy as jnp
from jax import lax

D = 6144
HIDDEN_SIZE = 8192
EXPERTS = 4
TOK_GRP = 64
CAP = 32
TOKENS = 2048
N_DP = 16
N_EXPERT = 32


def live_table(key):
    groups = TOKENS // TOK_GRP
    first_key, second_key = jax.random.split(key, 2)
    counted = jax.random.randint(first_key, (groups,), CAP, TOK_GRP + 1)
    order = jax.random.permutation(second_key, groups)
    return jnp.where(order == 0, TOK_GRP, counted).astype(jnp.int32)


def route_table(key, counted):
    groups = TOKENS // TOK_GRP
    slots = EXPERTS * CAP
    hot_key, group_key = jax.random.split(key, 2)
    hottest = jax.random.randint(hot_key, (), 0, EXPERTS)
    keys = jax.random.split(group_key, groups)

    def one_group(group_seed, count):
        key_a, key_b, key_c, key_d, key_e = jax.random.split(group_seed, 5)
        index = jnp.arange(slots, dtype=jnp.int32)
        owner = index // CAP
        scores = jax.random.randint(key_a, (slots,), 0, 1 << 16) * slots + index
        scores = jnp.where(owner == hottest, index - slots, scores)
        order = jnp.argsort(scores, stable=True)
        place = jnp.argsort(order, stable=True)
        chosen = place < 2 * count
        spot = jnp.cumsum(chosen.astype(jnp.int32)) - 1
        listed = jnp.zeros((2 * TOK_GRP,), jnp.int32).at[jnp.where(chosen, spot, 2 * TOK_GRP)].set(owner, mode='drop')
        rows = jnp.arange(TOK_GRP, dtype=jnp.int32)
        live_rows = rows < count
        token_score = jax.random.randint(key_b, (TOK_GRP,), 0, 1 << 16) * TOK_GRP + rows
        token_score = jnp.where(live_rows, token_score, (1 << 28) + rows)
        holder = jnp.argsort(token_score, stable=True)
        spare_first = jax.random.randint(key_c, (TOK_GRP,), 0, EXPERTS)
        spare_second = (spare_first + 1 + jax.random.randint(key_d, (TOK_GRP,), 0, EXPERTS - 1)) % EXPERTS
        listed_first = listed[rows]
        listed_second = listed[jnp.minimum(rows + count, 2 * TOK_GRP - 1)]
        flipped = jax.random.randint(key_e, (TOK_GRP,), 0, 2) == 1
        chosen_first = jnp.where(flipped, listed_second, listed_first)
        chosen_second = jnp.where(flipped, listed_first, listed_second)
        first = jnp.where(live_rows, chosen_first, spare_first)
        second = jnp.where(live_rows, chosen_second, spare_second)
        paired = jnp.stack([first, second], axis=1).astype(jnp.int32)
        return jnp.zeros((TOK_GRP, 2), jnp.int32).at[holder].set(paired)
    table = jax.vmap(one_group)(keys, counted)
    return table.reshape(TOKENS, 2)


def draw_expert_ids(key, part):
    counted = live_table(jax.random.fold_in(key, 7))
    return route_table(jax.random.fold_in(key, 8), counted)


def draw_live_counts(key, part):
    return live_table(jax.random.fold_in(key, 7))


def block_scale(rng, extent, cuts, least, largest):
    level = 1.0
    for axis_at, shards_of in cuts:
        heights = jax.random.uniform(jax.random.fold_in(jax.random.fold_in(rng, 6), axis_at), (shards_of,), jnp.float32, least / len(cuts), largest / len(cuts))
        level = level * jnp.repeat(jnp.exp(heights), extent[axis_at] // shards_of).reshape((-1,) + (1,) * (len(extent) - 1 - axis_at))
    return level


def bell_draw(stream_key, dims, scale, limit, shards=(), kind=jnp.bfloat16):
    values = jax.random.normal(stream_key, dims, jnp.float32) * scale
    if len(shards) > 0:
        values = block_scale(stream_key, dims, shards, -0.22, 0.18) * values
    return jnp.clip(values, min=-limit, max=limit).astype(kind)


def setup_inputs(seed: int = 0) -> dict:
    arg_keys = jax.random.split(jax.random.key(seed), 8)
    return {
        "inputs": bell_draw(arg_keys[0], (TOKENS, D), 1.0, 6.0, ((0, 32), (1, 16))),
        "grad_out": bell_draw(arg_keys[1], (TOKENS, D), 1.0, 6.0, ((0, 32), (1, 16))),
        "expert_ids": draw_expert_ids(jax.random.fold_in(arg_keys[7], 71), 0),
        "live_counts": draw_live_counts(jax.random.fold_in(arg_keys[7], 71), 0),
        "router_weight": bell_draw(arg_keys[4], (D, EXPERTS), D ** -0.5, 0.078125, ((0, 16),)),
        "up_weight": bell_draw(arg_keys[5], (D, EXPERTS * HIDDEN_SIZE), D ** -0.5, 0.078125, ((0, 16), (1, 32))),
        "down_weight": bell_draw(arg_keys[6], (D, EXPERTS * HIDDEN_SIZE), HIDDEN_SIZE ** -0.5, 0.0625, ((0, 16), (1, 32))),
    }


ROOT_HALF = 0.7071067811865476
INV_ROOT_TWO_PI = 0.3989422804014327


def gelu_value(value):
    return 0.5 * value * (1.0 + jax.scipy.special.erf(value * ROOT_HALF))


def gelu_slope(value):
    return 0.5 * (1.0 + jax.scipy.special.erf(value * ROOT_HALF)) + value * jnp.exp(-0.5 * value * value) * INV_ROOT_TWO_PI


def expert_pass(rows_in, rows_grad, gate_rows, up_matrix, down_matrix, pieces, column_parts):
    row_count = rows_in.shape[0]
    width, units = up_matrix.shape
    share = width // pieces
    part_width = units // column_parts

    def add_piece(carry, piece_index):
        before_sum, back_sum = carry
        start = piece_index * share
        rows_piece = lax.dynamic_slice_in_dim(rows_in, start, share, 1)
        grad_piece = lax.dynamic_slice_in_dim(rows_grad, start, share, 1)
        up_piece = lax.dynamic_slice_in_dim(up_matrix, start, share, 0)
        down_piece = lax.dynamic_slice_in_dim(down_matrix, start, share, 0)
        before_part = jnp.dot(rows_piece, up_piece, preferred_element_type=jnp.float32)
        back_part = jnp.dot(grad_piece, down_piece, preferred_element_type=jnp.float32)
        before_part = lax.optimization_barrier(before_part.astype(jnp.bfloat16)).astype(jnp.float32)
        back_part = lax.optimization_barrier(back_part.astype(jnp.bfloat16)).astype(jnp.float32)
        return (before_sum + before_part, back_sum + back_part), None

    empty = jnp.zeros((row_count, units), jnp.float32)
    sums, _ = lax.scan(add_piece, (empty, empty), jnp.arange(pieces, dtype=jnp.int32))
    before_act, back_act = sums
    active = gelu_value(before_act)
    hidden = lax.optimization_barrier(active.astype(jnp.bfloat16))
    gate_column = gate_rows.astype(jnp.float32)[:, None]
    product = hidden.astype(jnp.float32) * back_act
    gate_parts = jnp.sum(product.reshape(row_count, column_parts, part_width), axis=2)
    gate_total = jnp.sum(lax.optimization_barrier(gate_parts.astype(jnp.bfloat16)).astype(jnp.float32), axis=1)
    inner_grad = (gate_column * back_act * gelu_slope(before_act)).astype(jnp.bfloat16)
    weighted = (gate_column * active).astype(jnp.bfloat16)
    up_part = jnp.dot(rows_in.T, inner_grad, preferred_element_type=jnp.float32).astype(jnp.bfloat16)
    down_part = jnp.dot(rows_grad.T, weighted, preferred_element_type=jnp.float32).astype(jnp.bfloat16)
    inner_blocks = inner_grad.astype(jnp.float32).reshape(row_count, column_parts, part_width)
    up_blocks = up_matrix.astype(jnp.float32).reshape(width, column_parts, part_width)
    input_blocks = jnp.einsum("rgc,dgc->grd", inner_blocks, up_blocks, precision=lax.Precision.HIGHEST)
    input_sum = jnp.sum(lax.optimization_barrier(input_blocks.astype(jnp.bfloat16)).astype(jnp.float32), axis=0)
    return input_sum, gate_total, up_part, down_part


def reference(inputs, grad_out, expert_ids, live_counts, router_weight, up_weight, down_weight):
    groups = N_EXPERT
    pieces = N_DP
    per_group = TOK_GRP
    experts = EXPERTS
    capacity = CAP
    width = D
    units = HIDDEN_SIZE
    column_parts = groups // experts
    labels = jnp.arange(experts).astype(jnp.int32)
    logits = jnp.dot(inputs, router_weight, preferred_element_type=jnp.float32)
    first_hot = (expert_ids[:, 0:1] == labels[None, :]).astype(jnp.float32)
    second_hot = (expert_ids[:, 1:2] == labels[None, :]).astype(jnp.float32)
    logit_gap = jnp.sum(logits * (first_hot - second_hot), axis=1)
    gate_first = jax.nn.sigmoid(logit_gap).astype(jnp.bfloat16)
    gate_second = jax.nn.sigmoid(-logit_gap).astype(jnp.bfloat16)
    group_ids = expert_ids.reshape(groups, per_group, 2)
    pick_ids = jnp.concatenate([group_ids[:, :, 0], group_ids[:, :, 1]], axis=1)
    pick_gates = jnp.concatenate([gate_first.reshape(groups, per_group), gate_second.reshape(groups, per_group)], axis=1)
    position = (jnp.arange(2 * per_device_count(per_group)).astype(jnp.int32) % per_group).astype(jnp.int32)
    is_live = position[None, :] < live_counts[:, None]
    one_hot = ((pick_ids[:, :, None] == labels[None, None, :]) & is_live[:, :, None]).astype(jnp.int32)
    pick_rank = jnp.sum(jnp.cumsum(one_hot, axis=1) * one_hot, axis=2) - 1
    group_rows = groups * capacity
    overflow = experts * group_rows
    source = jnp.arange(groups).astype(jnp.int32)[:, None]
    flat_slot = jnp.where(is_live, pick_ids * group_rows + source * capacity + pick_rank, overflow).reshape(-1).astype(jnp.int32)
    token_index = (source * per_group + position[None, :]).reshape(-1).astype(jnp.int32)
    all_tokens = groups * per_group
    slot_table = jnp.full((overflow,), all_tokens, jnp.int32).at[flat_slot].set(token_index, mode="drop")
    gate_table = jnp.zeros((overflow,), jnp.bfloat16).at[flat_slot].set(pick_gates.reshape(-1), mode="drop")
    rows_all = jnp.take(inputs, slot_table, axis=0, mode="fill", fill_value=0).reshape(experts, group_rows, width)
    grads_all = jnp.take(grad_out, slot_table, axis=0, mode="fill", fill_value=0).reshape(experts, group_rows, width)

    def one_expert(items):
        rows_in, rows_grad, gate_rows, which = items
        start = which * units
        up_matrix = lax.dynamic_slice_in_dim(up_weight, start, units, 1)
        down_matrix = lax.dynamic_slice_in_dim(down_weight, start, units, 1)
        return expert_pass(rows_in, rows_grad, gate_rows, up_matrix, down_matrix, pieces, column_parts)

    input_sum, gate_total, up_part, down_part = lax.map(one_expert, (rows_all, grads_all, gate_table.reshape(experts, group_rows), labels))
    grad_up = up_part.transpose(1, 0, 2).reshape(width, experts * units)
    grad_down = down_part.transpose(1, 0, 2).reshape(width, experts * units)
    part_pick = jnp.take(input_sum.reshape(overflow, width), flat_slot, axis=0, mode="fill", fill_value=0).reshape(groups, 2 * per_group, width)
    gate_pick = jnp.take(gate_total.reshape(overflow), flat_slot, axis=0, mode="fill", fill_value=0).reshape(groups, 2 * per_group)
    gate_value = pick_gates.astype(jnp.float32)
    delta = lax.optimization_barrier((gate_pick * gate_value * (1.0 - gate_value)).astype(jnp.bfloat16)).astype(jnp.float32)
    delta_diff = (delta[:, :per_group] - delta[:, per_group:]).reshape(all_tokens)
    logit_grad = delta_diff[:, None] * (first_hot - second_hot)
    part_sum = (part_pick[:, :per_group] + part_pick[:, per_group:]).reshape(all_tokens, width)
    router_side = jnp.dot(logit_grad, router_weight.astype(jnp.float32).T, precision=lax.Precision.HIGHEST)
    grad_inputs = (grad_out.astype(jnp.float32) + part_sum + router_side).astype(jnp.bfloat16)
    grad_router = jnp.dot(inputs.astype(jnp.float32).T, logit_grad, precision=lax.Precision.HIGHEST)
    return (grad_inputs, grad_up, grad_down, grad_router)


def per_device_count(value):
    return value
```

```python
import jax
import jax.numpy as jnp
from jax import lax
from jax.experimental import pallas as pl
from jax.experimental.pallas import tpu as pltpu
from jax.sharding import PartitionSpec as P

MESH = pl.DeviceIdType.MESH
F32 = jnp.float32
BF16 = jnp.bfloat16
ROOT_HALF = 0.7071067811865476
INV_ROOT_TWO_PI = 0.3989422804014327

ORDERS = ((0, 2, 1, 3), (2, 1, 3, 0), (1, 3, 0, 2), (3, 0, 2, 1))
STEPS = 8
TICKS = 15
ROWS = 144
PARTS = ((0, 80), (80, 64))


def split(value):
    high = value.astype(BF16)
    return high, (value - high.astype(F32)).astype(BF16)


def dot(a, b, contract):
    return lax.dot_general(a, b, ((contract[:1], contract[1:]), ((), ())), preferred_element_type=F32)


def dot2(a, b, contract):
    high, low = split(a)
    return dot(high, b, contract) + dot(low, b, contract)


def route(a_row, b_row, expert):
    hit = jnp.where((a_row == expert) | (b_row == expert), 1.0, 0.0)
    upper = lax.broadcasted_iota(jnp.int32, (64, 64), 0) < lax.broadcasted_iota(jnp.int32, (64, 64), 1)
    rank = dot(
        jnp.broadcast_to(hit, (16, 64)).astype(BF16), jnp.where(upper, 1.0, 0.0).astype(BF16), (1, 0)
    )[0:1]
    slot = lax.broadcasted_iota(jnp.int32, (32, 64), 0).astype(F32)
    return jnp.where(slot == jnp.broadcast_to(rank, (32, 64)), jnp.broadcast_to(hit, (32, 64)), 0.0)


def signed_hot(a_row, b_row):
    row = lax.broadcasted_iota(jnp.int32, (16, 64), 0).astype(F32)
    first = jnp.where(row == jnp.broadcast_to(a_row, (16, 64)), 1.0, 0.0)
    second = jnp.where(row == jnp.broadcast_to(b_row, (16, 64)), 1.0, 0.0)
    return first - second


def kernel(
    x_ref, d_ref, meta_ref, rwt_ref, up_ref, down_ref,
    gi_ref, gu_ref, gd_ref, gr_ref,
    tb, pb, ph, ax, ad, part, rs0, rs1, rs2, ag, inn, wgt, pi, sx, rb, ret,
    ls, lr, gap, gaps, gp, gpr, gs, gret, dd, ddr,
    z_s, z_r, b_s, b_r, rs_s, rs_r, ag_s, ag_r, sx_s, sx_r, ret_s, ret_r,
    l_s, l_r, gap_s, gap_r, gp_s, gp_r, gr_s, gr_r, dd_s, dd_r,
):
    dp = lax.axis_index("dp")
    ex = lax.axis_index("expert")
    x, y = lax.rem(dp, 4), dp // 4
    z, c = ex // 2, lax.rem(ex, 2)
    expert = (z // 4).astype(F32)
    xe, ye = lax.rem((x + 1) // 2, 2), lax.rem((y + 1) // 2, 2)
    bits = (xe, x // 2, ye, y // 2)

    def partner(dims):
        px, py = x, y
        if 0 in dims:
            px = x + 1 - 2 * lax.rem(x, 2)
        if 1 in dims:
            px = 3 - x
        if 2 in dims:
            py = y + 1 - 2 * lax.rem(y, 2)
        if 3 in dims:
            py = 3 - y
        return (py * 4 + px, ex)

    sibling = (dp, z * 2 + 1 - c)
    above = (dp, lax.rem(z + 1, 16) * 2 + c)
    below = (dp, lax.rem(z + 15, 16) * 2 + c)

    def copy(src, dst, send, recv, device):
        return pltpu.make_async_remote_copy(
            src_ref=src, dst_ref=dst, send_sem=send, recv_sem=recv, device_id=device, device_id_type=MESH
        )

    def along_expert(i):
        return (dp, lax.rem(ex + i, 32)), lax.rem(ex + 32 - i, 32)

    def along_dp(i):
        return (lax.rem(dp + i, 16), ex), lax.rem(dp + 16 - i, 16)

    def spread(n, peer, source, table, mine, send, recv):
        def one(i, carry):
            device, _ = peer(i)
            copy(source(i), table.at[mine], send.at[i], recv.at[i], device).start()
            return carry

        lax.fori_loop(1, n, one, 0)

    def gather_wait(n, peer, source, table, send, recv):
        def one(i, carry):
            device, origin = peer(i)
            c = copy(source(i), table.at[origin], send.at[i], recv.at[i], device)
            c.wait_send()
            c.wait_recv()
            return carry

        lax.fori_loop(1, n, one, 0)

    barrier = pltpu.get_barrier_semaphore()

    def greet(i, carry):
        pl.semaphore_signal(barrier, inc=1, device_id=along_expert(i)[0], device_id_type=MESH)
        return carry

    def greet_dp(i, carry):
        pl.semaphore_signal(barrier, inc=1, device_id=along_dp(i)[0], device_id_type=MESH)
        return carry

    lax.fori_loop(1, 32, greet, 0)
    lax.fori_loop(1, 16, greet_dp, 0)

    tb[0, 0, c, 0:64] = x_ref[...]
    tb[0, 0, c, 64:80] = meta_ref[...]
    tb[0, 0, c, 80:144] = d_ref[...]
    a_own = meta_ref[0:8, 0:64].astype(F32)[0:1]
    b_own = meta_ref[8:16, 0:64].astype(F32)[0:1]
    ls[...] = jnp.zeros_like(ls)
    ls[:, 0:64] = dot(rwt_ref[...], x_ref[...], (1, 1))[0:8]
    gp[...] = jnp.zeros_like(gp)
    gap[...] = jnp.zeros_like(gap)
    dd[...] = jnp.zeros_like(dd)

    pl.semaphore_wait(barrier, 46)

    def z_copy(p, u, src, dst):
        low, size = PARTS[p]
        rows = pl.ds(low, size)
        return copy(
            tb.at[u if src is not None else 0, src if src is not None else 0, c, rows],
            tb.at[u, dst, c, rows],
            z_s.at[p, u, dst],
            z_r.at[p, u, dst],
            above if u == 0 else below,
        )

    def b_copy(p, u, j, core):
        low, size = PARTS[p]
        rows = pl.ds(low, size)
        return copy(tb.at[u, j, core, rows], tb.at[u, j, core, rows], b_s.at[p, u, j], b_r.at[p, u, j], sibling)

    for p in (0, 1):
        z_copy(p, 0, None, 1).start()
        z_copy(p, 1, None, 0).start()
        b_copy(p, 0, 0, c).start()
    spread(16, along_dp, lambda i: ls, lr, dp, l_s, l_r)
    lr[dp] = ls[...]
    for e in range(4):
        ph[e * 32 : e * 32 + 32, :] = route(a_own, b_own, float(e)).astype(BF16)

    def z_step(t, p):
        @pl.when(t < STEPS - 1)
        def _():
            z_copy(p, 0, t, t + 1).wait_recv()

            @pl.when(t < STEPS - 2)
            def _():
                z_copy(p, 0, t + 1, t + 2).start()

            b_copy(p, 0, t + 1, c).start()

        @pl.when(t < STEPS)
        def _():
            z_copy(p, 1, t, t).wait_recv()

            @pl.when(t < STEPS - 1)
            def _():
                z_copy(p, 1, t, t + 1).start()

            b_copy(p, 1, t, c).start()

    def z_sent(t, p):
        @pl.when((t > 0) & (t < STEPS))
        def _():
            z_copy(p, 0, t - 1, t).wait_send()

        @pl.when((t > 0) & (t < STEPS + 1))
        def _():
            z_copy(p, 1, t - 1, t - 1).wait_send()

    def info(q):
        order = ORDERS[q]
        return order, tuple(bits[d] for d in order)

    def rs_sem(which, j, q, m):
        return which.at[j, q * 5 + m]

    def rs_copy(j, q, m):
        order, b = info(q)
        if m == 0:
            src, dst = part.at[j, q, pl.ds((1 - b[0]) * 8, 8)], rs0.at[j, q]
            dims = order[:1]
        elif m == 1:
            src, dst = part.at[j, q, pl.ds(b[0] * 8 + (1 - b[1]) * 4, 4)], rs1.at[j, q]
            dims = order[1:2]
        else:
            mask = m - 1
            src = part.at[j, q, pl.ds(b[0] * 8 + b[1] * 4 + local(b, mask), 1)]
            dst = rs2.at[j, q, pl.ds(mask - 1, 1)]
            dims = tuple(d for k, d in enumerate(order[2:]) if mask & (2 >> k))
        return copy(src, dst, rs_sem(rs_s, j, q, m), rs_sem(rs_r, j, q, m), partner(dims))

    def local(b, mask):
        high = 1 - b[2] if mask & 2 else b[2]
        low = 1 - b[3] if mask & 1 else b[3]
        return high * 2 + low

    def ag_copy(j, q, m, arriving=False):
        order, b = info(q)
        if m == 0:
            dims, size = order[:1], 8
            start = ((1 - b[0]) if arriving else b[0]) * 8
        elif m == 1:
            dims, size = order[1:2], 4
            start = b[0] * 8 + ((1 - b[1]) if arriving else b[1]) * 4
        else:
            mask = m - 1
            dims, size = tuple(d for k, d in enumerate(order[2:]) if mask & (2 >> k)), 1
            start = b[0] * 8 + b[1] * 4 + local(b, mask if arriving else 0)
        ref = ag.at[j, q, pl.ds(start, size)]
        return copy(ref, ref, rs_sem(ag_s, j, q, m), rs_sem(ag_r, j, q, m), partner(dims))

    def start_unit(u, j):
        up, down = up_ref[...], down_ref[...]
        xs, ds = [], []
        for core in (0, 1):
            rows = tb.at[u, j, core]
            meta = rows[64:80, 0:64].astype(F32)
            pick = route(meta[0:1], meta[8:9], expert).astype(BF16)
            pb[u, j, core] = pick
            xs.append(dot(pick, rows[0:64], (1, 0)).astype(BF16))
            ds.append(dot(pick, rows[80:144], (1, 0)).astype(BF16))
            ax[j, core * 64 + u * 32 : core * 64 + u * 32 + 32] = xs[core]
            ad[j, core * 64 + u * 32 : core * 64 + u * 32 + 32] = ds[core]
        for a, (rows, weight) in enumerate(((xs, up), (ds, down))):
            q = 2 * u + a
            value = dot(jnp.concatenate(rows, axis=0), weight, (1, 0)).astype(BF16)
            for block in range(16):
                bit = (block >> 3 & 1, block >> 2 & 1, block >> 1 & 1, block & 1)
                spot = sum(bit[d] << (3 - k) for k, d in enumerate(ORDERS[q]))
                half, column = bit[0], bit[1] * 4 + bit[2] * 2 + bit[3]
                part[j, q, spot] = value[half * 32 : half * 32 + 32, column * 128 : column * 128 + 128]
            rs_copy(j, q, 0).start()

    def wait_sibling(u, j):
        for p in (0, 1):
            cp = b_copy(p, u, j, 1 - c)
            cp.wait_send()
            cp.wait_recv()

    def reduce_one(j):
        for q in range(4):
            _, b = info(q)
            rs_copy(j, q, 0).wait_recv()
            near = (1 - b[1]) * 4
            part[j, q, pl.ds(b[0] * 8 + near, 4)] += rs0[j, q, pl.ds(near, 4)]
            rs_copy(j, q, 1).start()
            near = b[1] * 4
            part[j, q, pl.ds(b[0] * 8 + near, 4)] += rs0[j, q, pl.ds(near, 4)]
            rs_copy(j, q, 0).wait_send()

    def reduce_two(j):
        for q in range(4):
            _, b = info(q)
            rs_copy(j, q, 1).wait_recv()
            for mask in (3, 1, 2, 0):
                at = local(b, mask)
                part[j, q, b[0] * 8 + b[1] * 4 + at] += rs1[j, q, at]
                if mask:
                    rs_copy(j, q, mask + 1).start()
            rs_copy(j, q, 1).wait_send()

    def chip_of(u, j):
        return lax.rem(z + 16 - j, 16) if u == 0 else lax.rem(z + j + 1, 16)

    def total(j, q):
        _, b = info(q)
        for mask in (1, 2, 3):
            rs_copy(j, q, mask + 1).wait_recv()
            rs_copy(j, q, mask + 1).wait_send()
        parts = rs2[j, q].astype(F32)
        own = part[j, q, b[0] * 8 + b[1] * 4 + b[2] * 2 + b[3]].astype(F32)
        return own + parts[0] + parts[1] + parts[2]

    def activate(j):
        for u in (0, 1):
            d = chip_of(u, j)
            before = total(j, 2 * u)
            back = total(j, 2 * u + 1)
            meta = tb[u, j, xe, 64:80, 0:64].astype(F32)
            gap_row = gaps[2 * d + xe][:, 0:64]
            gate_row = jnp.where(
                meta[0:1] == expert,
                jax.nn.sigmoid(gap_row),
                jnp.where(meta[8:9] == expert, jax.nn.sigmoid(-gap_row), 0.0),
            )
            gate_row = gate_row.astype(BF16).astype(F32)
            gate = jnp.sum(pb[u, j, xe].astype(F32) * jnp.broadcast_to(gate_row, (32, 64)), axis=1, keepdims=True)
            bell = 0.5 * (1.0 + lax.erf(before * ROOT_HALF))
            active = before * bell
            slope = bell + before * jnp.exp(-0.5 * before * before) * INV_ROOT_TWO_PI
            inner = (gate * back * slope).astype(BF16)
            weighted = (gate * active).astype(BF16)
            product = active.astype(BF16).astype(F32) * back
            for a, tile in ((0, inner), (1, weighted)):
                q = 2 * u + a
                _, b = info(q)
                ag[j, q, b[0] * 8 + b[1] * 4 + b[2] * 2 + b[3]] = tile
                for mask in (3, 1, 2):
                    ag_copy(j, q, mask + 1).start()
            high, low = split(product)
            ones = jnp.ones((16, 128), BF16)
            sums = dot(ones, high, (1, 1)) + dot(ones, low, (1, 1))
            gp[d, :, 0:32] = sums[0:1]

    def gather_one(j):
        for q in range(4):
            for mask in (1, 2, 3):
                ag_copy(j, q, mask + 1, True).wait_recv()
            ag_copy(j, q, 1).start()
            for mask in (1, 2, 3):
                ag_copy(j, q, mask + 1).wait_send()

    def gather_two(j):
        for q in range(4):
            ag_copy(j, q, 1, True).wait_recv()
            ag_copy(j, q, 0).start()
            ag_copy(j, q, 1).wait_send()

    def sx_copy(j):
        return copy(pi.at[j, 1 - c], sx.at[j], sx_s.at[j], sx_r.at[j], sibling)

    def finish_unit(j):
        for q in range(4):
            ag_copy(j, q, 0, True).wait_recv()
            ag_copy(j, q, 0).wait_send()
            u, into = q // 2, (inn, wgt)[q % 2]
            for block in range(16):
                bit = (block >> 3 & 1, block >> 2 & 1, block >> 1 & 1, block & 1)
                spot = sum(bit[d] << (3 - k) for k, d in enumerate(ORDERS[q]))
                row, column = bit[0] * 64 + u * 32, (bit[1] * 4 + bit[2] * 2 + bit[3]) * 128
                into[j, row : row + 32, column : column + 128] = ag[j, q, spot]
        value = dot(inn[j], up_ref[...], (1, 1)).astype(BF16)
        pi[j, 0] = value[0:64]
        pi[j, 1] = value[64:128]
        sx_copy(j).start()

    def ret_copy(u, j):
        device = (dp, chip_of(u, j) * 2 + c)
        return copy(rb.at[j, pl.ds(u * 32, 32)], ret.at[z], ret_s.at[u, j], ret_r.at[u, j], device)

    def return_unit(j):
        sx_copy(j).wait_recv()
        sx_copy(j).wait_send()
        rb[j] = (pi[j, c].astype(F32) + sx[j].astype(F32)).astype(BF16)

        @pl.when(j == 0)
        def _():
            ret[z] = rb[0, 0:32]

        @pl.when(j > 0)
        def _():
            ret_copy(0, j).start()

        ret_copy(1, j).start()

    def tick(t, carry):
        def stage(lag, action):
            @pl.when((t >= lag) & (t < lag + STEPS))
            def _():
                action(t - lag)

        @pl.when(t < STEPS)
        def _():
            wait_sibling(0, t)
            start_unit(0, t)

        z_step(t, 0)
        z_sent(t, 0)

        @pl.when(t == 1)
        def _():
            gather_wait(16, along_dp, lambda i: ls, lr, l_s, l_r)
            logits = jnp.sum(lr[...], axis=0)
            hot = signed_hot(a_own, b_own)[0:8]
            gap[:, 0:64] = jnp.sum(logits[:, 0:64] * hot, axis=0, keepdims=True)
            gaps[ex] = gap[...]
            spread(32, along_expert, lambda i: gap, gaps, ex, gap_s, gap_r)

        @pl.when(t == 3)
        def _():
            gather_wait(32, along_expert, lambda i: gap, gaps, gap_s, gap_r)

        stage(7, return_unit)
        stage(5, gather_two)
        stage(4, gather_one)
        stage(3, activate)

        @pl.when(t == 10)
        def _():
            gpr[dp] = gp[...]
            spread(16, along_dp, lambda i: gp, gpr, dp, gp_s, gp_r)

        stage(2, reduce_two)
        stage(1, reduce_one)
        z_step(t, 1)
        z_sent(t, 1)

        @pl.when(t == 12)
        def _():
            gather_wait(16, along_dp, lambda i: gp, gpr, gp_s, gp_r)
            for half in (0, 1):
                mine = [k for k in range(16) if ((k % 4 + 1) // 2) % 2 == half]
                acc = gpr[mine[0]]
                for k in mine[1:]:
                    acc = acc + gpr[k]
                for k in range(16):
                    gs[2 * k + half] = acc[k].astype(BF16).astype(F32)
            gret[ex] = gs[ex]
            spread(32, along_expert, lambda i: gs.at[along_expert(i)[0][1]], gret, ex, gr_s, gr_r)

        stage(6, finish_unit)

        @pl.when(t < STEPS)
        def _():
            wait_sibling(1, t)
            start_unit(1, t)

        @pl.when(t == 14)
        def _():
            gather_wait(32, along_expert, lambda i: gs.at[along_expert(i)[0][1]], gret, gr_s, gr_r)
            picked = []
            for e in range(4):
                row = gret[8 * e]
                for k in range(1, 8):
                    row = row + gret[8 * e + k]
                row = jnp.broadcast_to(row[:, 0:32], (16, 32))
                picked.append(dot2(row, ph[e * 32 : e * 32 + 32, :], (1, 0))[0:1])
            first = jnp.zeros((1, 64), F32)
            second = jnp.zeros((1, 64), F32)
            for e in range(4):
                first = first + jnp.where(a_own == float(e), picked[e], 0.0)
                second = second + jnp.where(b_own == float(e), picked[e], 0.0)
            row = gap[:, 0:64]
            gate0 = jax.nn.sigmoid(row).astype(BF16).astype(F32)
            gate1 = jax.nn.sigmoid(-row).astype(BF16).astype(F32)
            delta0 = (first * gate0 * (1.0 - gate0)).astype(BF16).astype(F32)
            delta1 = (second * gate1 * (1.0 - gate1)).astype(BF16).astype(F32)
            dd[:, 0:64] = delta0 - delta1
            ddr[ex] = dd[...]
            spread(32, along_expert, lambda i: dd, ddr, ex, dd_s, dd_r)

        return carry

    lax.fori_loop(0, TICKS, tick, 0)

    rows = STEPS * 128
    for source, values, out in ((ax, inn, gu_ref), (ad, wgt, gd_ref)):
        out[...] = dot(source[...].reshape(rows, 384), values[...].reshape(rows, 1024), (0, 0)).astype(BF16)

    gather_wait(32, along_expert, lambda i: dd, ddr, dd_s, dd_r)

    def add_router(k, acc):
        for u in (0, 1):
            d = chip_of(u, k)
            for core in (0, 1):
                meta = tb[u, k, core, 64:80, 0:64].astype(F32)
                grad = signed_hot(meta[0:1], meta[8:9]) * jnp.broadcast_to(ddr[2 * d + core][:, 0:64], (16, 64))
                acc = acc + dot2(grad, tb[u, k, core, 0:64], (1, 0))
        return acc

    gr_ref[...] = lax.fori_loop(0, STEPS, add_router, jnp.zeros((16, 384), F32))

    def returned(j, carry):
        @pl.when(j > 0)
        def _():
            cp = ret_copy(0, j)
            cp.wait_send()
            cp.wait_recv()

        cp = ret_copy(1, j)
        cp.wait_send()
        cp.wait_recv()
        return carry

    lax.fori_loop(0, STEPS, returned, 0)
    sums = []
    for e in range(4):
        acc = ret[4 * e].astype(F32)
        for k in range(1, 4):
            acc = acc + ret[4 * e + k].astype(F32)
        sums.append(acc)
    high, low = split(jnp.concatenate(sums, axis=0))
    pick = ph[...]
    value = d_ref[...].astype(F32) + (dot(pick, high, (0, 0)) + dot(pick, low, (0, 0)))
    high, low = split(signed_hot(a_own, b_own) * jnp.broadcast_to(dd[:, 0:64], (16, 64)))
    weight = rwt_ref[...]
    value = value + (dot(high, weight, (0, 0)) + dot(low, weight, (0, 0)))
    gi_ref[...] = value.astype(BF16)


def local(inputs, grad_out, expert_ids, live_counts, router_weight, up_weight, down_weight):
    live = jnp.arange(64, dtype=jnp.int32)[:, None] < live_counts[0]
    ids = jnp.where(live, expert_ids, -1).astype(BF16).T
    meta = jnp.full((16, 384), -1.0, BF16).at[0, 0:64].set(ids[0]).at[8, 0:64].set(ids[1])
    router = jnp.zeros((16, 384), BF16).at[0:4].set(router_weight.T)
    vmem = pl.BlockSpec(memory_space=pltpu.VMEM)
    dma = pltpu.SemaphoreType.DMA
    grads = jax.ShapeDtypeStruct((384, 1024), BF16)
    grad_inputs, grad_up, grad_down, grad_router = pl.pallas_call(
        kernel,
        out_shape=(jax.ShapeDtypeStruct((64, 384), BF16), grads, grads, jax.ShapeDtypeStruct((16, 384), F32)),
        in_specs=[vmem] * 6,
        out_specs=(vmem,) * 4,
        scratch_shapes=[
            pltpu.VMEM((2, STEPS, 2, ROWS, 384), BF16),
            pltpu.VMEM((2, STEPS, 2, 32, 64), BF16),
            pltpu.VMEM((128, 64), BF16),
            pltpu.VMEM((STEPS, 128, 384), BF16),
            pltpu.VMEM((STEPS, 128, 384), BF16),
            pltpu.VMEM((STEPS, 4, 16, 32, 128), BF16),
            pltpu.VMEM((STEPS, 4, 8, 32, 128), BF16),
            pltpu.VMEM((STEPS, 4, 4, 32, 128), BF16),
            pltpu.VMEM((STEPS, 4, 3, 32, 128), BF16),
            pltpu.VMEM((STEPS, 4, 16, 32, 128), BF16),
            pltpu.VMEM((STEPS, 128, 1024), BF16),
            pltpu.VMEM((STEPS, 128, 1024), BF16),
            pltpu.VMEM((STEPS, 2, 64, 384), BF16),
            pltpu.VMEM((STEPS, 64, 384), BF16),
            pltpu.VMEM((STEPS, 64, 384), BF16),
            pltpu.VMEM((16, 32, 384), BF16),
            pltpu.VMEM((8, 128), F32),
            pltpu.VMEM((16, 8, 128), F32),
            pltpu.VMEM((1, 128), F32),
            pltpu.VMEM((32, 1, 128), F32),
            pltpu.VMEM((16, 1, 128), F32),
            pltpu.VMEM((16, 16, 1, 128), F32),
            pltpu.VMEM((32, 1, 128), F32),
            pltpu.VMEM((32, 1, 128), F32),
            pltpu.VMEM((1, 128), F32),
            pltpu.VMEM((32, 1, 128), F32),
            dma((2, 2, STEPS)), dma((2, 2, STEPS)),
            dma((2, 2, STEPS)), dma((2, 2, STEPS)),
            dma((STEPS, 20)), dma((STEPS, 20)),
            dma((STEPS, 20)), dma((STEPS, 20)),
            dma((STEPS,)), dma((STEPS,)),
            dma((2, STEPS)), dma((2, STEPS)),
            dma((16,)), dma((16,)),
            dma((32,)), dma((32,)),
            dma((16,)), dma((16,)),
            dma((32,)), dma((32,)),
            dma((32,)), dma((32,)),
        ],
        compiler_params=pltpu.CompilerParams(
            collective_id=0, has_side_effects=True, vmem_limit_bytes=56 * 2**20
        ),
        name="moe_backward",
    )(inputs, grad_out, meta, router, up_weight, down_weight)
    return grad_inputs, grad_up, grad_down, grad_router[0:4].T


def solution(mesh):
    placed = (
        P("expert", "dp"),
        P("expert", "dp"),
        P("expert", None),
        P("expert"),
        P("dp", None),
        P("dp", "expert"),
        P("dp", "expert"),
    )
    return jax.shard_map(
        local,
        mesh=mesh,
        in_specs=placed,
        out_specs=(P("expert", "dp"), P("dp", "expert"), P("dp", "expert"), P("dp", None)),
        check_vma=False,
    )
```

```python
import jax
import jax.numpy as jnp
from jax import lax
from jax.experimental import pallas as pl
from jax.experimental.pallas import tpu as pltpu
from jax.sharding import PartitionSpec as P

MESH = pl.DeviceIdType.MESH
F32 = jnp.float32
BF16 = jnp.bfloat16
ROOT_HALF = 0.7071067811865476
INV_ROOT_TWO_PI = 0.3989422804014327

ORDERS = ((0, 2, 1, 3), (2, 1, 3, 0), (1, 3, 0, 2), (3, 0, 2, 1))
STEPS = 8
TICKS = 15
ROWS = 144
PARTS = ((0, 80), (80, 64))


def split(value):
    high = value.astype(BF16)
    return high, (value - high.astype(F32)).astype(BF16)


def dot(a, b, contract):
    return lax.dot_general(a, b, ((contract[:1], contract[1:]), ((), ())), preferred_element_type=F32)


def dot2(a, b, contract):
    high, low = split(a)
    return dot(high, b, contract) + dot(low, b, contract)


def route(pairs):
    row = lax.broadcasted_iota(jnp.int32, (16, 64), 0)
    hits = [jnp.where((a == e) | (b == e), 1.0, 0.0) for a, b, e in pairs]
    table = jnp.zeros((16, 64), F32)
    for k, hit in enumerate(hits):
        table = jnp.where(row == k, jnp.broadcast_to(hit, (16, 64)), table)
    upper = lax.broadcasted_iota(jnp.int32, (64, 64), 0) < lax.broadcasted_iota(jnp.int32, (64, 64), 1)
    rank = dot(table.astype(BF16), jnp.where(upper, 1.0, 0.0).astype(BF16), (1, 0))
    slot = lax.broadcasted_iota(jnp.int32, (32, 64), 0).astype(F32)
    picks = []
    for k, hit in enumerate(hits):
        at = jnp.broadcast_to(rank[k : k + 1], (32, 64))
        picks.append(jnp.where(slot == at, jnp.broadcast_to(hit, (32, 64)), 0.0).astype(BF16))
    return picks


def signed_hot(a_row, b_row):
    row = lax.broadcasted_iota(jnp.int32, (16, 64), 0).astype(F32)
    first = jnp.where(row == jnp.broadcast_to(a_row, (16, 64)), 1.0, 0.0)
    second = jnp.where(row == jnp.broadcast_to(b_row, (16, 64)), 1.0, 0.0)
    return first - second


def kernel(
    x_hbm, d_hbm, ids_ref, live_ref, rwt_ref, up_hbm, down_hbm,
    gi_hbm, gu_hbm, gd_hbm, gr_hbm,
    up_ref, down_ref, rw, gi, gu, gd, gr, tb, pb, ph, ax, ad, part, rs0, rs1, rs2, ag, inn, wgt, pi, sx, rb, ret,
    ls, lr, gap, gaps, gp, gpr, gs, gret, dd, ddr,
    z_s, z_r, b_s, b_r, rs_s, rs_r, ag_s, ag_r, sx_s, sx_r, ret_s, ret_r,
    l_s, l_r, gap_s, gap_r, gp_s, gp_r, gr_s, gr_r, dd_s, dd_r, in_s, out_s,
):
    dp = lax.axis_index("dp")
    ex = lax.axis_index("expert")
    x, y = lax.rem(dp, 4), dp // 4
    z, c = ex // 2, lax.rem(ex, 2)
    expert = (z // 4).astype(F32)
    xe, ye = lax.rem((x + 1) // 2, 2), lax.rem((y + 1) // 2, 2)
    bits = (xe, x // 2, ye, y // 2)

    def partner(dims):
        px, py = x, y
        if 0 in dims:
            px = x + 1 - 2 * lax.rem(x, 2)
        if 1 in dims:
            px = 3 - x
        if 2 in dims:
            py = y + 1 - 2 * lax.rem(y, 2)
        if 3 in dims:
            py = 3 - y
        return (py * 4 + px, ex)

    sibling = (dp, z * 2 + 1 - c)
    above = (dp, lax.rem(z + 1, 16) * 2 + c)
    below = (dp, lax.rem(z + 15, 16) * 2 + c)

    def copy(src, dst, send, recv, device):
        return pltpu.make_async_remote_copy(
            src_ref=src, dst_ref=dst, send_sem=send, recv_sem=recv, device_id=device, device_id_type=MESH
        )

    def along_expert(i):
        return (dp, lax.rem(ex + i, 32)), lax.rem(ex + 32 - i, 32)

    def along_dp(i):
        return (lax.rem(dp + i, 16), ex), lax.rem(dp + 16 - i, 16)

    def spread(n, peer, source, table, mine, send, recv):
        def one(i, carry):
            device, _ = peer(i)
            copy(source(i), table.at[mine], send.at[i], recv.at[i], device).start()
            return carry

        lax.fori_loop(1, n, one, 0)

    def gather_wait(n, peer, source, table, send, recv):
        def one(i, carry):
            device, origin = peer(i)
            c = copy(source(i), table.at[origin], send.at[i], recv.at[i], device)
            c.wait_send()
            c.wait_recv()
            return carry

        lax.fori_loop(1, n, one, 0)

    loads = [
        pltpu.make_async_copy(src, dst, in_s.at[k])
        for k, (src, dst) in enumerate(
            (
                (x_hbm, tb.at[0, 0, c, pl.ds(0, 64)]),
                (d_hbm, tb.at[0, 0, c, pl.ds(80, 64)]),
                (up_hbm, up_ref),
                (down_hbm, down_ref),
            )
        )
    ]
    for load in loads:
        load.start()
    barrier = pltpu.get_barrier_semaphore()

    def greet(i, carry):
        pl.semaphore_signal(barrier, inc=1, device_id=along_expert(i)[0], device_id_type=MESH)
        return carry

    def greet_dp(i, carry):
        pl.semaphore_signal(barrier, inc=1, device_id=along_dp(i)[0], device_id_type=MESH)
        return carry

    lax.fori_loop(1, 32, greet, 0)
    lax.fori_loop(1, 16, greet_dp, 0)

    ids = ids_ref[...].astype(F32)
    alive = lax.broadcasted_iota(jnp.int32, (1, 64), 1) < live_ref[0]
    a_own = jnp.where(alive, ids[0:1], -1.0)
    b_own = jnp.where(alive, ids[1:2], -1.0)
    tb[0, 0, c, 64:80] = jnp.zeros((16, 384), BF16)
    low_half = lax.broadcasted_iota(jnp.int32, (16, 64), 0) < 8
    both = jnp.where(low_half, jnp.broadcast_to(a_own, (16, 64)), jnp.broadcast_to(b_own, (16, 64)))
    tb[0, 0, c, 64:80, 0:64] = both.astype(BF16)
    rw[...] = jnp.zeros_like(rw)
    rw[0:4] = rwt_ref[...]
    ls[...] = jnp.zeros_like(ls)
    for load in loads[0:2]:
        load.wait()
    ls[:, 0:64] = dot(rw[...], tb[0, 0, c, 0:64], (1, 1))[0:8]
    gp[...] = jnp.zeros_like(gp)
    gap[...] = jnp.zeros_like(gap)
    dd[...] = jnp.zeros_like(dd)

    pl.semaphore_wait(barrier, 46)

    def z_copy(p, u, src, dst):
        low, size = PARTS[p]
        rows = pl.ds(low, size)
        return copy(
            tb.at[u if src is not None else 0, src if src is not None else 0, c, rows],
            tb.at[u, dst, c, rows],
            z_s.at[p, u, dst],
            z_r.at[p, u, dst],
            above if u == 0 else below,
        )

    def b_copy(p, u, j, core):
        low, size = PARTS[p]
        rows = pl.ds(low, size)
        return copy(tb.at[u, j, core, rows], tb.at[u, j, core, rows], b_s.at[p, u, j], b_r.at[p, u, j], sibling)

    for p in (0, 1):
        z_copy(p, 0, None, 1).start()
        z_copy(p, 1, None, 0).start()
        b_copy(p, 0, 0, c).start()
    spread(16, along_dp, lambda i: ls, lr, dp, l_s, l_r)
    lr[dp] = ls[...]
    for e, pick in enumerate(route([(a_own, b_own, float(e)) for e in range(4)])):
        ph[e * 32 : e * 32 + 32, :] = pick

    def z_step(t, p):
        @pl.when(t < STEPS - 1)
        def _():
            z_copy(p, 0, t, t + 1).wait_recv()

            @pl.when(t < STEPS - 2)
            def _():
                z_copy(p, 0, t + 1, t + 2).start()

            b_copy(p, 0, t + 1, c).start()

        @pl.when(t < STEPS)
        def _():
            z_copy(p, 1, t, t).wait_recv()

            @pl.when(t < STEPS - 1)
            def _():
                z_copy(p, 1, t, t + 1).start()

            b_copy(p, 1, t, c).start()

    def z_sent(t, p):
        @pl.when((t > 0) & (t < STEPS))
        def _():
            z_copy(p, 0, t - 1, t).wait_send()

        @pl.when((t > 0) & (t < STEPS + 1))
        def _():
            z_copy(p, 1, t - 1, t - 1).wait_send()

    def info(q):
        order = ORDERS[q]
        return order, tuple(bits[d] for d in order)

    def rs_sem(which, j, q, m):
        return which.at[j, q * 5 + m]

    def rs_copy(j, q, m):
        order, b = info(q)
        if m == 0:
            src, dst = part.at[j, q, pl.ds((1 - b[0]) * 8, 8)], rs0.at[j, q]
            dims = order[:1]
        elif m == 1:
            src, dst = part.at[j, q, pl.ds(b[0] * 8 + (1 - b[1]) * 4, 4)], rs1.at[j, q]
            dims = order[1:2]
        else:
            mask = m - 1
            src = part.at[j, q, pl.ds(b[0] * 8 + b[1] * 4 + local(b, mask), 1)]
            dst = rs2.at[j, q, pl.ds(mask - 1, 1)]
            dims = tuple(d for k, d in enumerate(order[2:]) if mask & (2 >> k))
        return copy(src, dst, rs_sem(rs_s, j, q, m), rs_sem(rs_r, j, q, m), partner(dims))

    def local(b, mask):
        high = 1 - b[2] if mask & 2 else b[2]
        low = 1 - b[3] if mask & 1 else b[3]
        return high * 2 + low

    def ag_copy(j, q, m, arriving=False):
        order, b = info(q)
        if m == 0:
            dims, size = order[:1], 8
            start = ((1 - b[0]) if arriving else b[0]) * 8
        elif m == 1:
            dims, size = order[1:2], 4
            start = b[0] * 8 + ((1 - b[1]) if arriving else b[1]) * 4
        else:
            mask = m - 1
            dims, size = tuple(d for k, d in enumerate(order[2:]) if mask & (2 >> k)), 1
            start = b[0] * 8 + b[1] * 4 + local(b, mask if arriving else 0)
        ref = ag.at[j, q, pl.ds(start, size)]
        return copy(ref, ref, rs_sem(ag_s, j, q, m), rs_sem(ag_r, j, q, m), partner(dims))

    def start_units(j):
        keys = [(u, core) for core in (0, 1) for u in (0, 1)]
        for u in (0, 1):
            wait_sibling(u, j)
        pairs = []
        for u, core in keys:
            meta = tb[u, j, core, 64:80, 0:64].astype(F32)
            pairs.append((meta[0:1], meta[8:9], expert))
        picks = route(pairs)
        for (u, core), pick in zip(keys, picks):
            pb[u, j, core] = pick
        for a, (low, weight, keep) in enumerate(((0, up_ref, ax), (80, down_ref, ad))):
            rows = [
                dot(pick, tb[u, j, core, low : low + 64], (1, 0)).astype(BF16)
                for (u, core), pick in zip(keys, picks)
            ]
            rows = jnp.concatenate(rows, axis=0)
            keep[j] = rows
            value = dot(rows, weight[...], (1, 0)).astype(BF16)
            for u in (0, 1):
                q = 2 * u + a
                for block in range(16):
                    bit = (block >> 3 & 1, block >> 2 & 1, block >> 1 & 1, block & 1)
                    spot = sum(bit[d] << (3 - k) for k, d in enumerate(ORDERS[q]))
                    row, column = bit[0] * 64 + u * 32, (bit[1] * 4 + bit[2] * 2 + bit[3]) * 128
                    part[j, q, spot] = value[row : row + 32, column : column + 128]
                rs_copy(j, q, 0).start()

    def wait_sibling(u, j):
        for p in (0, 1):
            cp = b_copy(p, u, j, 1 - c)
            cp.wait_send()
            cp.wait_recv()

    def reduce_one(j):
        for q in range(4):
            _, b = info(q)
            rs_copy(j, q, 0).wait_recv()
            near = (1 - b[1]) * 4
            part[j, q, pl.ds(b[0] * 8 + near, 4)] += rs0[j, q, pl.ds(near, 4)]
            rs_copy(j, q, 1).start()
            near = b[1] * 4
            part[j, q, pl.ds(b[0] * 8 + near, 4)] += rs0[j, q, pl.ds(near, 4)]
            rs_copy(j, q, 0).wait_send()

    def reduce_two(j):
        for q in range(4):
            _, b = info(q)
            rs_copy(j, q, 1).wait_recv()
            for mask in (3, 1, 2, 0):
                at = local(b, mask)
                part[j, q, b[0] * 8 + b[1] * 4 + at] += rs1[j, q, at]
                if mask:
                    rs_copy(j, q, mask + 1).start()
            rs_copy(j, q, 1).wait_send()

    def chip_of(u, j):
        return lax.rem(z + 16 - j, 16) if u == 0 else lax.rem(z + j + 1, 16)

    def total(j, q):
        _, b = info(q)
        parts = rs2[j, q].astype(F32)
        own = part[j, q, b[0] * 8 + b[1] * 4 + b[2] * 2 + b[3]].astype(F32)
        return own + parts[0] + parts[1] + parts[2]

    def activate(j):
        for q in range(4):
            for mask in (1, 2, 3):
                rs_copy(j, q, mask + 1).wait_recv()
        before = jnp.concatenate([total(j, 0), total(j, 2)], axis=0)
        back = jnp.concatenate([total(j, 1), total(j, 3)], axis=0)
        gates = []
        for u in (0, 1):
            meta = tb[u, j, xe, 64:80, 0:64].astype(F32)
            gap_row = gaps[2 * chip_of(u, j) + xe][:, 0:64]
            gate_row = jnp.where(
                meta[0:1] == expert,
                jax.nn.sigmoid(gap_row),
                jnp.where(meta[8:9] == expert, jax.nn.sigmoid(-gap_row), 0.0),
            )
            gate_row = gate_row.astype(BF16).astype(F32)
            gates.append(
                jnp.sum(pb[u, j, xe].astype(F32) * jnp.broadcast_to(gate_row, (32, 64)), axis=1, keepdims=True)
            )
        gate = jnp.concatenate(gates, axis=0)
        bell = 0.5 * (1.0 + lax.erf(before * ROOT_HALF))
        active = before * bell
        slope = bell + before * jnp.exp(-0.5 * before * before) * INV_ROOT_TWO_PI
        inner = (gate * back * slope).astype(BF16)
        weighted = (gate * active).astype(BF16)
        product = active.astype(BF16).astype(F32) * back
        high, low = split(product)
        ones = jnp.ones((16, 128), BF16)
        sums = dot(ones, high, (1, 1)) + dot(ones, low, (1, 1))
        for q in range(4):
            _, b = info(q)
            u, tile = q // 2, (inner, weighted)[q % 2]
            ag[j, q, b[0] * 8 + b[1] * 4 + b[2] * 2 + b[3]] = tile[u * 32 : u * 32 + 32]
        for q in range(4):
            for mask in (3, 1, 2):
                ag_copy(j, q, mask + 1).start()
        for u in (0, 1):
            gp[chip_of(u, j), :, 0:32] = sums[0:1, u * 32 : u * 32 + 32]
        for q in range(4):
            for mask in (1, 2, 3):
                rs_copy(j, q, mask + 1).wait_send()

    def gather_one(j):
        for q in range(4):
            for mask in (1, 2, 3):
                ag_copy(j, q, mask + 1, True).wait_recv()
            ag_copy(j, q, 1).start()
            for mask in (1, 2, 3):
                ag_copy(j, q, mask + 1).wait_send()

    def gather_two(j):
        for q in range(4):
            ag_copy(j, q, 1, True).wait_recv()
            ag_copy(j, q, 0).start()
            ag_copy(j, q, 1).wait_send()

    def sx_copy(j):
        return copy(pi.at[j, 1 - c], sx.at[j], sx_s.at[j], sx_r.at[j], sibling)

    def finish_unit(j):
        for q in range(4):
            ag_copy(j, q, 0, True).wait_recv()
            ag_copy(j, q, 0).wait_send()
            u, into = q // 2, (inn, wgt)[q % 2]
            for block in range(16):
                bit = (block >> 3 & 1, block >> 2 & 1, block >> 1 & 1, block & 1)
                spot = sum(bit[d] << (3 - k) for k, d in enumerate(ORDERS[q]))
                row, column = bit[0] * 64 + u * 32, (bit[1] * 4 + bit[2] * 2 + bit[3]) * 128
                into[j, row : row + 32, column : column + 128] = ag[j, q, spot]
        value = dot(inn[j], up_ref[...], (1, 1)).astype(BF16)
        pi[j, 0] = value[0:64]
        pi[j, 1] = value[64:128]
        sx_copy(j).start()

    def ret_copy(u, j):
        device = (dp, chip_of(u, j) * 2 + c)
        return copy(rb.at[j, pl.ds(u * 32, 32)], ret.at[z], ret_s.at[u, j], ret_r.at[u, j], device)

    def return_unit(j):
        sx_copy(j).wait_recv()
        sx_copy(j).wait_send()
        rb[j] = (pi[j, c].astype(F32) + sx[j].astype(F32)).astype(BF16)

        @pl.when(j == 0)
        def _():
            ret[z] = rb[0, 0:32]

        @pl.when(j > 0)
        def _():
            ret_copy(0, j).start()

        ret_copy(1, j).start()

    def tick(t, carry):
        def stage(lag, action):
            @pl.when((t >= lag) & (t < lag + STEPS))
            def _():
                action(t - lag)

        stage(0, start_units)
        z_step(t + 1, 0)
        z_sent(t + 1, 0)
        stage(1, reduce_one)
        stage(2, reduce_two)

        @pl.when(t == 0)
        def _():
            gather_wait(16, along_dp, lambda i: ls, lr, l_s, l_r)
            logits = jnp.sum(lr[...], axis=0)
            hot = signed_hot(a_own, b_own)[0:8]
            gap[:, 0:64] = jnp.sum(logits[:, 0:64] * hot, axis=0, keepdims=True)
            gaps[ex] = gap[...]
            spread(32, along_expert, lambda i: gap, gaps, ex, gap_s, gap_r)

        @pl.when(t == 3)
        def _():
            gather_wait(32, along_expert, lambda i: gap, gaps, gap_s, gap_r)

        stage(3, activate)
        z_step(t + 1, 1)
        z_sent(t + 1, 1)

        @pl.when(t == 10)
        def _():
            gpr[dp] = gp[...]
            spread(16, along_dp, lambda i: gp, gpr, dp, gp_s, gp_r)

        stage(4, gather_one)
        stage(5, gather_two)
        stage(6, finish_unit)
        stage(7, return_unit)

        @pl.when(t == 11)
        def _():
            gather_wait(16, along_dp, lambda i: gp, gpr, gp_s, gp_r)
            for half in (0, 1):
                mine = [k for k in range(16) if ((k % 4 + 1) // 2) % 2 == half]
                acc = gpr[mine[0]]
                for k in mine[1:]:
                    acc = acc + gpr[k]
                for k in range(16):
                    gs[2 * k + half] = acc[k].astype(BF16).astype(F32)
            gret[ex] = gs[ex]
            spread(32, along_expert, lambda i: gs.at[along_expert(i)[0][1]], gret, ex, gr_s, gr_r)

        @pl.when(t == 13)
        def _():
            gather_wait(32, along_expert, lambda i: gs.at[along_expert(i)[0][1]], gret, gr_s, gr_r)
            picked = []
            for e in range(4):
                row = gret[8 * e]
                for k in range(1, 8):
                    row = row + gret[8 * e + k]
                row = jnp.broadcast_to(row[:, 0:32], (16, 32))
                picked.append(dot2(row, ph[e * 32 : e * 32 + 32, :], (1, 0))[0:1])
            first = jnp.zeros((1, 64), F32)
            second = jnp.zeros((1, 64), F32)
            for e in range(4):
                first = first + jnp.where(a_own == float(e), picked[e], 0.0)
                second = second + jnp.where(b_own == float(e), picked[e], 0.0)
            row = gap[:, 0:64]
            gate0 = jax.nn.sigmoid(row).astype(BF16).astype(F32)
            gate1 = jax.nn.sigmoid(-row).astype(BF16).astype(F32)
            delta0 = (first * gate0 * (1.0 - gate0)).astype(BF16).astype(F32)
            delta1 = (second * gate1 * (1.0 - gate1)).astype(BF16).astype(F32)
            dd[:, 0:64] = delta0 - delta1
            ddr[ex] = dd[...]
            spread(32, along_expert, lambda i: dd, ddr, ex, dd_s, dd_r)

        return carry

    for load in loads[2:]:
        load.wait()
    for p in (0, 1):
        z_step(0, p)
    lax.fori_loop(0, TICKS, tick, 0)

    rows = STEPS * 128
    stores = [
        pltpu.make_async_copy(src, dst, out_s.at[k])
        for k, (src, dst) in enumerate(((gu, gu_hbm), (gd, gd_hbm), (gr, gr_hbm), (gi, gi_hbm)))
    ]
    for k, (source, values, out) in enumerate(((ax, inn, gu), (ad, wgt, gd))):
        out[...] = dot(source[...].reshape(rows, 384), values[...].reshape(rows, 1024), (0, 0)).astype(BF16)
        stores[k].start()

    gather_wait(32, along_expert, lambda i: dd, ddr, dd_s, dd_r)

    def add_router(k, acc):
        for u in (0, 1):
            d = chip_of(u, k)
            for core in (0, 1):
                meta = tb[u, k, core, 64:80, 0:64].astype(F32)
                grad = signed_hot(meta[0:1], meta[8:9]) * jnp.broadcast_to(ddr[2 * d + core][:, 0:64], (16, 64))
                acc = acc + dot2(grad, tb[u, k, core, 0:64], (1, 0))
        return acc

    gr[...] = lax.fori_loop(0, STEPS, add_router, jnp.zeros((16, 384), F32))[0:4]
    stores[2].start()

    def returned(j, carry):
        @pl.when(j > 0)
        def _():
            cp = ret_copy(0, j)
            cp.wait_send()
            cp.wait_recv()

        cp = ret_copy(1, j)
        cp.wait_send()
        cp.wait_recv()
        return carry

    lax.fori_loop(0, STEPS, returned, 0)
    sums = []
    for e in range(4):
        acc = ret[4 * e].astype(F32)
        for k in range(1, 4):
            acc = acc + ret[4 * e + k].astype(F32)
        sums.append(acc)
    high, low = split(jnp.concatenate(sums, axis=0))
    pick = ph[...]
    value = tb[0, 0, c, 80:144].astype(F32) + (dot(pick, high, (0, 0)) + dot(pick, low, (0, 0)))
    high, low = split(signed_hot(a_own, b_own) * jnp.broadcast_to(dd[:, 0:64], (16, 64)))
    weight = rw[...]
    value = value + (dot(high, weight, (0, 0)) + dot(low, weight, (0, 0)))
    gi[...] = value.astype(BF16)
    stores[3].start()
    for store in stores:
        store.wait()


def place(*refs):
    sources, outs, held, (arrive, leave) = refs[:4], refs[4:8], refs[8:12], refs[12:]
    pieces = [(1, 0, 192), (1, 192, 192), (2, 0, 192), (2, 192, 192), (0, 0, 64), (3, 0, 4)]
    loads, stores = [], []
    for n, (k, low, size) in enumerate(pieces):
        rows = pl.ds(low, size)
        loads.append(pltpu.make_async_copy(sources[k].at[rows], held[k].at[rows], arrive.at[n]))
        stores.append(pltpu.make_async_copy(held[k].at[rows], outs[k].at[rows], leave.at[n]))
    for load in loads:
        load.start()
    for load, store in zip(loads, stores):
        load.wait()
        store.start()
    for store in stores:
        store.wait()


def local(inputs, grad_out, expert_ids, live_counts, router_weight, up_weight, down_weight):
    vmem = pl.BlockSpec(memory_space=pltpu.VMEM)
    dma = pltpu.SemaphoreType.DMA
    anywhere = pl.BlockSpec(memory_space=pl.ANY)
    grads = jax.ShapeDtypeStruct((384, 1024), BF16)
    shapes = (jax.ShapeDtypeStruct((64, 384), BF16), grads, grads, jax.ShapeDtypeStruct((4, 384), F32))
    results = pl.pallas_call(
        kernel,
        out_shape=shapes,
        in_specs=[anywhere, anywhere, vmem, pl.BlockSpec(memory_space=pltpu.SMEM), vmem, anywhere, anywhere],
        out_specs=(anywhere,) * 4,
        scratch_shapes=[
            pltpu.VMEM((384, 1024), BF16),
            pltpu.VMEM((384, 1024), BF16),
            pltpu.VMEM((16, 384), BF16),
            pltpu.VMEM((64, 384), BF16),
            pltpu.VMEM((384, 1024), BF16),
            pltpu.VMEM((384, 1024), BF16),
            pltpu.VMEM((4, 384), F32),
            pltpu.VMEM((2, STEPS, 2, ROWS, 384), BF16),
            pltpu.VMEM((2, STEPS, 2, 32, 64), BF16),
            pltpu.VMEM((128, 64), BF16),
            pltpu.VMEM((STEPS, 128, 384), BF16),
            pltpu.VMEM((STEPS, 128, 384), BF16),
            pltpu.VMEM((STEPS, 4, 16, 32, 128), BF16),
            pltpu.VMEM((STEPS, 4, 8, 32, 128), BF16),
            pltpu.VMEM((STEPS, 4, 4, 32, 128), BF16),
            pltpu.VMEM((STEPS, 4, 3, 32, 128), BF16),
            pltpu.VMEM((STEPS, 4, 16, 32, 128), BF16),
            pltpu.VMEM((STEPS, 128, 1024), BF16),
            pltpu.VMEM((STEPS, 128, 1024), BF16),
            pltpu.VMEM((STEPS, 2, 64, 384), BF16),
            pltpu.VMEM((STEPS, 64, 384), BF16),
            pltpu.VMEM((STEPS, 64, 384), BF16),
            pltpu.VMEM((16, 32, 384), BF16),
            pltpu.VMEM((8, 128), F32),
            pltpu.VMEM((16, 8, 128), F32),
            pltpu.VMEM((1, 128), F32),
            pltpu.VMEM((32, 1, 128), F32),
            pltpu.VMEM((16, 1, 128), F32),
            pltpu.VMEM((16, 16, 1, 128), F32),
            pltpu.VMEM((32, 1, 128), F32),
            pltpu.VMEM((32, 1, 128), F32),
            pltpu.VMEM((1, 128), F32),
            pltpu.VMEM((32, 1, 128), F32),
            dma((2, 2, STEPS)), dma((2, 2, STEPS)),
            dma((2, 2, STEPS)), dma((2, 2, STEPS)),
            dma((STEPS, 20)), dma((STEPS, 20)),
            dma((STEPS, 20)), dma((STEPS, 20)),
            dma((STEPS,)), dma((STEPS,)),
            dma((2, STEPS)), dma((2, STEPS)),
            dma((16,)), dma((16,)),
            dma((32,)), dma((32,)),
            dma((16,)), dma((16,)),
            dma((32,)), dma((32,)),
            dma((32,)), dma((32,)),
            dma((4,)), dma((4,)),
        ],
        compiler_params=pltpu.CompilerParams(
            collective_id=0, has_side_effects=True, vmem_limit_bytes=56 * 2**20
        ),
        name="moe_backward",
    )(inputs, grad_out, expert_ids.T, live_counts, router_weight.T, up_weight, down_weight)
    grad_inputs, grad_up, grad_down, grad_router = pl.pallas_call(
        place,
        out_shape=shapes,
        in_specs=[anywhere] * 4,
        out_specs=(anywhere,) * 4,
        scratch_shapes=[pltpu.VMEM(shape.shape, shape.dtype) for shape in shapes] + [dma((6,)), dma((6,))],
        name="place",
    )(*results)
    return grad_inputs, grad_up, grad_down, grad_router.T


def solution(mesh):
    placed = (
        P("expert", "dp"),
        P("expert", "dp"),
        P("expert", None),
        P("expert"),
        P("dp", None),
        P("dp", "expert"),
        P("dp", "expert"),
    )
    return jax.shard_map(
        local,
        mesh=mesh,
        in_specs=placed,
        out_specs=(P("expert", "dp"), P("dp", "expert"), P("dp", "expert"), P("dp", None)),
        check_vma=False,
    )
```

```python
import jax
import jax.numpy as jnp
from jax import lax
from jax.experimental import pallas as pl
from jax.experimental.pallas import tpu as pltpu
from jax.sharding import PartitionSpec as P

MESH = pl.DeviceIdType.MESH
F32 = jnp.float32
BF16 = jnp.bfloat16
ROOT_HALF = 0.7071067811865476
INV_ROOT_TWO_PI = 0.3989422804014327

ORDERS = ((0, 2, 1, 3), (2, 1, 3, 0), (1, 3, 0, 2), (3, 0, 2, 1))
STEPS = 8
TICKS = 15
ROWS = 144
PARTS = ((0, 80), (80, 64))


def split(value):
    high = value.astype(BF16)
    return high, (value - high.astype(F32)).astype(BF16)


def dot(a, b, contract):
    return lax.dot_general(a, b, ((contract[:1], contract[1:]), ((), ())), preferred_element_type=F32)


def dot2(a, b, contract):
    high, low = split(a)
    return dot(high, b, contract) + dot(low, b, contract)


def route(pairs):
    row = lax.broadcasted_iota(jnp.int32, (16, 64), 0)
    hits = [jnp.where((a == e) | (b == e), 1.0, 0.0) for a, b, e in pairs]
    table = jnp.zeros((16, 64), F32)
    for k, hit in enumerate(hits):
        table = jnp.where(row == k, jnp.broadcast_to(hit, (16, 64)), table)
    upper = lax.broadcasted_iota(jnp.int32, (64, 64), 0) < lax.broadcasted_iota(jnp.int32, (64, 64), 1)
    rank = dot(table.astype(BF16), jnp.where(upper, 1.0, 0.0).astype(BF16), (1, 0))
    slot = lax.broadcasted_iota(jnp.int32, (32, 64), 0).astype(F32)
    picks = []
    for k, hit in enumerate(hits):
        at = jnp.broadcast_to(rank[k : k + 1], (32, 64))
        picks.append(jnp.where(slot == at, jnp.broadcast_to(hit, (32, 64)), 0.0).astype(BF16))
    return picks


def signed_hot(a_row, b_row):
    row = lax.broadcasted_iota(jnp.int32, (16, 64), 0).astype(F32)
    first = jnp.where(row == jnp.broadcast_to(a_row, (16, 64)), 1.0, 0.0)
    second = jnp.where(row == jnp.broadcast_to(b_row, (16, 64)), 1.0, 0.0)
    return first - second


def kernel(
    x_hbm, d_hbm, ids_ref, live_ref, rwt_ref, up_hbm, down_hbm,
    gi_hbm, gu_hbm, gd_hbm, gr_hbm,
    up_ref, down_ref, rw, gi, gu, gd, gr, tb, pb, ph, ax, ad, part, rs0, rs1, rs2, ag, inn, wgt, pi, sx, rb, ret,
    ls, lr, gap, gaps, gp, gpr, gs, gret, dd, ddr,
    z_s, z_r, b_s, b_r, rs_s, rs_r, ag_s, ag_r, sx_s, sx_r, ret_s, ret_r,
    l_s, l_r, gap_s, gap_r, gp_s, gp_r, gr_s, gr_r, dd_s, dd_r, in_s, out_s,
):
    dp = lax.axis_index("dp")
    ex = lax.axis_index("expert")
    x, y = lax.rem(dp, 4), dp // 4
    z, c = ex // 2, lax.rem(ex, 2)
    expert = (z // 4).astype(F32)
    xe, ye = lax.rem((x + 1) // 2, 2), lax.rem((y + 1) // 2, 2)
    bits = (xe, x // 2, ye, y // 2)

    def partner(dims):
        px, py = x, y
        if 0 in dims:
            px = x + 1 - 2 * lax.rem(x, 2)
        if 1 in dims:
            px = 3 - x
        if 2 in dims:
            py = y + 1 - 2 * lax.rem(y, 2)
        if 3 in dims:
            py = 3 - y
        return (py * 4 + px, ex)

    sibling = (dp, z * 2 + 1 - c)
    above = (dp, lax.rem(z + 1, 16) * 2 + c)
    below = (dp, lax.rem(z + 15, 16) * 2 + c)

    def copy(src, dst, send, recv, device):
        return pltpu.make_async_remote_copy(
            src_ref=src, dst_ref=dst, send_sem=send, recv_sem=recv, device_id=device, device_id_type=MESH
        )

    def along_expert(i):
        return (dp, lax.rem(ex + i, 32)), lax.rem(ex + 32 - i, 32)

    def along_dp(i):
        return (lax.rem(dp + i, 16), ex), lax.rem(dp + 16 - i, 16)

    def spread(n, peer, source, table, mine, send, recv):
        def one(i, carry):
            device, _ = peer(i)
            copy(source(i), table.at[mine], send.at[i], recv.at[i], device).start()
            return carry

        lax.fori_loop(1, n, one, 0)

    def gather_wait(n, peer, source, table, send, recv):
        def one(i, carry):
            device, origin = peer(i)
            c = copy(source(i), table.at[origin], send.at[i], recv.at[i], device)
            c.wait_send()
            c.wait_recv()
            return carry

        lax.fori_loop(1, n, one, 0)

    loads = [
        pltpu.make_async_copy(src, dst, in_s.at[k])
        for k, (src, dst) in enumerate(
            (
                (x_hbm, tb.at[0, 0, c, pl.ds(0, 64)]),
                (d_hbm, tb.at[0, 0, c, pl.ds(80, 64)]),
                (up_hbm, up_ref),
                (down_hbm, down_ref),
            )
        )
    ]
    for load in loads:
        load.start()
    barrier = pltpu.get_barrier_semaphore()

    def greet_dp(i, carry):
        pl.semaphore_signal(barrier, inc=1, device_id=along_dp(i)[0], device_id_type=MESH)
        return carry

    for device in (above, below, sibling):
        pl.semaphore_signal(barrier, inc=1, device_id=device, device_id_type=MESH)
    lax.fori_loop(1, 16, greet_dp, 0)

    ids = ids_ref[...].astype(F32)
    alive = lax.broadcasted_iota(jnp.int32, (1, 64), 1) < live_ref[0]
    a_own = jnp.where(alive, ids[0:1], -1.0)
    b_own = jnp.where(alive, ids[1:2], -1.0)
    tb[0, 0, c, 64:80] = jnp.zeros((16, 384), BF16)
    low_half = lax.broadcasted_iota(jnp.int32, (16, 64), 0) < 8
    both = jnp.where(low_half, jnp.broadcast_to(a_own, (16, 64)), jnp.broadcast_to(b_own, (16, 64)))
    tb[0, 0, c, 64:80, 0:64] = both.astype(BF16)
    rw[...] = jnp.zeros_like(rw)
    rw[0:4] = rwt_ref[...]
    ls[...] = jnp.zeros_like(ls)
    for load in loads[0:2]:
        load.wait()
    ls[:, 0:64] = dot(rw[...], tb[0, 0, c, 0:64], (1, 1))[0:8]
    gp[...] = jnp.zeros_like(gp)
    gap[...] = jnp.zeros_like(gap)
    dd[...] = jnp.zeros_like(dd)

    pl.semaphore_wait(barrier, 18)

    def z_copy(p, u, src, dst):
        low, size = PARTS[p]
        rows = pl.ds(low, size)
        return copy(
            tb.at[u if src is not None else 0, src if src is not None else 0, c, rows],
            tb.at[u, dst, c, rows],
            z_s.at[p, u, dst],
            z_r.at[p, u, dst],
            above if u == 0 else below,
        )

    def b_copy(p, u, j, core):
        low, size = PARTS[p]
        rows = pl.ds(low, size)
        return copy(tb.at[u, j, core, rows], tb.at[u, j, core, rows], b_s.at[p, u, j], b_r.at[p, u, j], sibling)

    for p in (0, 1):
        z_copy(p, 0, None, 1).start()
        z_copy(p, 1, None, 0).start()
        b_copy(p, 0, 0, c).start()
    spread(16, along_dp, lambda i: ls, lr, dp, l_s, l_r)
    lr[dp] = ls[...]
    for e, pick in enumerate(route([(a_own, b_own, float(e)) for e in range(4)])):
        ph[e * 32 : e * 32 + 32, :] = pick

    def z_step(t, p):
        @pl.when(t < STEPS - 1)
        def _():
            z_copy(p, 0, t, t + 1).wait_recv()

            @pl.when(t < STEPS - 2)
            def _():
                z_copy(p, 0, t + 1, t + 2).start()

            b_copy(p, 0, t + 1, c).start()

        @pl.when(t < STEPS)
        def _():
            z_copy(p, 1, t, t).wait_recv()

            @pl.when(t < STEPS - 1)
            def _():
                z_copy(p, 1, t, t + 1).start()

            b_copy(p, 1, t, c).start()

    def z_sent(t, p):
        @pl.when((t > 0) & (t < STEPS))
        def _():
            z_copy(p, 0, t - 1, t).wait_send()

        @pl.when((t > 0) & (t < STEPS + 1))
        def _():
            z_copy(p, 1, t - 1, t - 1).wait_send()

    def info(q):
        order = ORDERS[q]
        return order, tuple(bits[d] for d in order)

    def rs_sem(which, j, q, m):
        return which.at[j, q * 5 + m]

    def rs_copy(j, q, m):
        order, b = info(q)
        if m == 0:
            src, dst = part.at[j, q, pl.ds((1 - b[0]) * 8, 8)], rs0.at[j, q]
            dims = order[:1]
        elif m == 1:
            src, dst = part.at[j, q, pl.ds(b[0] * 8 + (1 - b[1]) * 4, 4)], rs1.at[j, q]
            dims = order[1:2]
        else:
            mask = m - 1
            src = part.at[j, q, pl.ds(b[0] * 8 + b[1] * 4 + local(b, mask), 1)]
            dst = rs2.at[j, q, pl.ds(mask - 1, 1)]
            dims = tuple(d for k, d in enumerate(order[2:]) if mask & (2 >> k))
        return copy(src, dst, rs_sem(rs_s, j, q, m), rs_sem(rs_r, j, q, m), partner(dims))

    def local(b, mask):
        high = 1 - b[2] if mask & 2 else b[2]
        low = 1 - b[3] if mask & 1 else b[3]
        return high * 2 + low

    def ag_copy(j, q, m, arriving=False):
        order, b = info(q)
        if m == 0:
            dims, size = order[:1], 8
            start = ((1 - b[0]) if arriving else b[0]) * 8
        elif m == 1:
            dims, size = order[1:2], 4
            start = b[0] * 8 + ((1 - b[1]) if arriving else b[1]) * 4
        else:
            mask = m - 1
            dims, size = tuple(d for k, d in enumerate(order[2:]) if mask & (2 >> k)), 1
            start = b[0] * 8 + b[1] * 4 + local(b, mask if arriving else 0)
        ref = ag.at[j, q, pl.ds(start, size)]
        return copy(ref, ref, rs_sem(ag_s, j, q, m), rs_sem(ag_r, j, q, m), partner(dims))

    def start_units(j):
        keys = [(u, core) for core in (0, 1) for u in (0, 1)]
        for u in (0, 1):
            wait_sibling(u, j)
        pairs = []
        for u, core in keys:
            meta = tb[u, j, core, 64:80, 0:64].astype(F32)
            pairs.append((meta[0:1], meta[8:9], expert))
        picks = route(pairs)
        for (u, core), pick in zip(keys, picks):
            pb[u, j, core] = pick
        for a, (low, weight, keep) in enumerate(((0, up_ref, ax), (80, down_ref, ad))):
            rows = [
                dot(pick, tb[u, j, core, low : low + 64], (1, 0)).astype(BF16)
                for (u, core), pick in zip(keys, picks)
            ]
            rows = jnp.concatenate(rows, axis=0)
            keep[j] = rows
            value = dot(rows, weight[...], (1, 0)).astype(BF16)
            for u in (0, 1):
                q = 2 * u + a
                for block in range(16):
                    bit = (block >> 3 & 1, block >> 2 & 1, block >> 1 & 1, block & 1)
                    spot = sum(bit[d] << (3 - k) for k, d in enumerate(ORDERS[q]))
                    row, column = bit[0] * 64 + u * 32, (bit[1] * 4 + bit[2] * 2 + bit[3]) * 128
                    part[j, q, spot] = value[row : row + 32, column : column + 128]
                rs_copy(j, q, 0).start()

    def wait_sibling(u, j):
        for p in (0, 1):
            cp = b_copy(p, u, j, 1 - c)
            cp.wait_send()
            cp.wait_recv()

    def reduce_one(j):
        for q in range(4):
            _, b = info(q)
            rs_copy(j, q, 0).wait_recv()
            near = (1 - b[1]) * 4
            part[j, q, pl.ds(b[0] * 8 + near, 4)] += rs0[j, q, pl.ds(near, 4)]
            rs_copy(j, q, 1).start()
            near = b[1] * 4
            part[j, q, pl.ds(b[0] * 8 + near, 4)] += rs0[j, q, pl.ds(near, 4)]
            rs_copy(j, q, 0).wait_send()

    def reduce_two(j):
        for q in range(4):
            _, b = info(q)
            rs_copy(j, q, 1).wait_recv()
            for mask in (3, 1, 2, 0):
                at = local(b, mask)
                part[j, q, b[0] * 8 + b[1] * 4 + at] += rs1[j, q, at]
                if mask:
                    rs_copy(j, q, mask + 1).start()
            rs_copy(j, q, 1).wait_send()

    def chip_of(u, j):
        return lax.rem(z + 16 - j, 16) if u == 0 else lax.rem(z + j + 1, 16)

    def total(j, q):
        _, b = info(q)
        parts = rs2[j, q].astype(F32)
        own = part[j, q, b[0] * 8 + b[1] * 4 + b[2] * 2 + b[3]].astype(F32)
        return own + parts[0] + parts[1] + parts[2]

    def gap_copy(u, j, core):
        target = lax.rem(z + j, 16) if u == 0 else lax.rem(z + 15 - j, 16)
        return copy(gap, gaps.at[ex], gap_s.at[u, j, core], gap_r.at[u, j], (dp, target * 2 + core))

    def gap_wait(u, j):
        origin = chip_of(u, j) * 2 + xe
        copy(gap, gaps.at[origin], gap_s.at[u, j, 0], gap_r.at[u, j], sibling).wait_recv()

    def activate(j):
        @pl.when((j > 0) | (c != xe))
        def _():
            gap_wait(0, j)

        gap_wait(1, j)
        for q in range(4):
            for mask in (1, 2, 3):
                rs_copy(j, q, mask + 1).wait_recv()
        before = jnp.concatenate([total(j, 0), total(j, 2)], axis=0)
        back = jnp.concatenate([total(j, 1), total(j, 3)], axis=0)
        gates = []
        for u in (0, 1):
            meta = tb[u, j, xe, 64:80, 0:64].astype(F32)
            gap_row = gaps[2 * chip_of(u, j) + xe][:, 0:64]
            gate_row = jnp.where(
                meta[0:1] == expert,
                jax.nn.sigmoid(gap_row),
                jnp.where(meta[8:9] == expert, jax.nn.sigmoid(-gap_row), 0.0),
            )
            gate_row = gate_row.astype(BF16).astype(F32)
            gates.append(
                jnp.sum(pb[u, j, xe].astype(F32) * jnp.broadcast_to(gate_row, (32, 64)), axis=1, keepdims=True)
            )
        gate = jnp.concatenate(gates, axis=0)
        bell = 0.5 * (1.0 + lax.erf(before * ROOT_HALF))
        active = before * bell
        slope = bell + before * jnp.exp(-0.5 * before * before) * INV_ROOT_TWO_PI
        inner = (gate * back * slope).astype(BF16)
        weighted = (gate * active).astype(BF16)
        product = active.astype(BF16).astype(F32) * back
        high, low = split(product)
        ones = jnp.ones((16, 128), BF16)
        sums = dot(ones, high, (1, 1)) + dot(ones, low, (1, 1))
        for q in range(4):
            _, b = info(q)
            u, tile = q // 2, (inner, weighted)[q % 2]
            ag[j, q, b[0] * 8 + b[1] * 4 + b[2] * 2 + b[3]] = tile[u * 32 : u * 32 + 32]
        for q in range(4):
            for mask in (3, 1, 2):
                ag_copy(j, q, mask + 1).start()
        for u in (0, 1):
            gp[chip_of(u, j), :, 0:32] = sums[0:1, u * 32 : u * 32 + 32]
        for q in range(4):
            for mask in (1, 2, 3):
                rs_copy(j, q, mask + 1).wait_send()

    def gather_one(j):
        for q in range(4):
            for mask in (1, 2, 3):
                ag_copy(j, q, mask + 1, True).wait_recv()
            ag_copy(j, q, 1).start()
            for mask in (1, 2, 3):
                ag_copy(j, q, mask + 1).wait_send()

    def gather_two(j):
        for q in range(4):
            ag_copy(j, q, 1, True).wait_recv()
            ag_copy(j, q, 0).start()
            ag_copy(j, q, 1).wait_send()

    def sx_copy(j):
        return copy(pi.at[j, 1 - c], sx.at[j], sx_s.at[j], sx_r.at[j], sibling)

    def finish_unit(j):
        for q in range(4):
            ag_copy(j, q, 0, True).wait_recv()
            ag_copy(j, q, 0).wait_send()
            u, into = q // 2, (inn, wgt)[q % 2]
            for block in range(16):
                bit = (block >> 3 & 1, block >> 2 & 1, block >> 1 & 1, block & 1)
                spot = sum(bit[d] << (3 - k) for k, d in enumerate(ORDERS[q]))
                row, column = bit[0] * 64 + u * 32, (bit[1] * 4 + bit[2] * 2 + bit[3]) * 128
                into[j, row : row + 32, column : column + 128] = ag[j, q, spot]
        value = dot(inn[j], up_ref[...], (1, 1)).astype(BF16)
        pi[j, 0] = value[0:64]
        pi[j, 1] = value[64:128]
        sx_copy(j).start()

    def ret_copy(u, j):
        device = (dp, chip_of(u, j) * 2 + c)
        return copy(rb.at[j, pl.ds(u * 32, 32)], ret.at[z], ret_s.at[u, j], ret_r.at[u, j], device)

    def return_unit(j):
        sx_copy(j).wait_recv()
        sx_copy(j).wait_send()
        rb[j] = (pi[j, c].astype(F32) + sx[j].astype(F32)).astype(BF16)

        @pl.when(j == 0)
        def _():
            ret[z] = rb[0, 0:32]

        @pl.when(j > 0)
        def _():
            ret_copy(0, j).start()

        ret_copy(1, j).start()

    def tick(t, carry):
        def stage(lag, action):
            @pl.when((t >= lag) & (t < lag + STEPS))
            def _():
                action(t - lag)

        stage(0, start_units)
        z_step(t + 1, 0)
        z_sent(t + 1, 0)
        stage(1, reduce_one)
        stage(2, reduce_two)

        @pl.when(t == 0)
        def _():
            gather_wait(16, along_dp, lambda i: ls, lr, l_s, l_r)
            logits = jnp.sum(lr[...], axis=0)
            hot = signed_hot(a_own, b_own)[0:8]
            gap[:, 0:64] = jnp.sum(logits[:, 0:64] * hot, axis=0, keepdims=True)
            gaps[ex] = gap[...]

        @pl.when((c == xe) & (t < STEPS))
        def _():
            for core in (0, 1):
                @pl.when((t > 0) | (core != c))
                def _():
                    gap_copy(0, t, core).start()

        @pl.when((c == xe) & (t > 0) & (t < STEPS + 1))
        def _():
            for core in (0, 1):
                gap_copy(1, t - 1, core).start()

        stage(3, activate)
        z_step(t + 1, 1)
        z_sent(t + 1, 1)

        @pl.when(t == 10)
        def _():
            gpr[dp] = gp[...]
            spread(16, along_dp, lambda i: gp, gpr, dp, gp_s, gp_r)

        stage(4, gather_one)
        stage(5, gather_two)
        stage(6, finish_unit)
        stage(7, return_unit)

        @pl.when(t == 11)
        def _():
            gather_wait(16, along_dp, lambda i: gp, gpr, gp_s, gp_r)
            for half in (0, 1):
                mine = [k for k in range(16) if ((k % 4 + 1) // 2) % 2 == half]
                acc = gpr[mine[0]]
                for k in mine[1:]:
                    acc = acc + gpr[k]
                for k in range(16):
                    gs[2 * k + half] = acc[k].astype(BF16).astype(F32)
            gret[ex] = gs[ex]
            spread(32, along_expert, lambda i: gs.at[along_expert(i)[0][1]], gret, ex, gr_s, gr_r)

        @pl.when(t == 13)
        def _():
            gather_wait(32, along_expert, lambda i: gs.at[along_expert(i)[0][1]], gret, gr_s, gr_r)
            picked = []
            for e in range(4):
                row = gret[8 * e]
                for k in range(1, 8):
                    row = row + gret[8 * e + k]
                row = jnp.broadcast_to(row[:, 0:32], (16, 32))
                picked.append(dot2(row, ph[e * 32 : e * 32 + 32, :], (1, 0))[0:1])
            first = jnp.zeros((1, 64), F32)
            second = jnp.zeros((1, 64), F32)
            for e in range(4):
                first = first + jnp.where(a_own == float(e), picked[e], 0.0)
                second = second + jnp.where(b_own == float(e), picked[e], 0.0)
            row = gap[:, 0:64]
            gate0 = jax.nn.sigmoid(row).astype(BF16).astype(F32)
            gate1 = jax.nn.sigmoid(-row).astype(BF16).astype(F32)
            delta0 = (first * gate0 * (1.0 - gate0)).astype(BF16).astype(F32)
            delta1 = (second * gate1 * (1.0 - gate1)).astype(BF16).astype(F32)
            dd[:, 0:64] = delta0 - delta1
            ddr[ex] = dd[...]
            spread(32, along_expert, lambda i: dd, ddr, ex, dd_s, dd_r)

        return carry

    for load in loads[2:]:
        load.wait()
    for p in (0, 1):
        z_step(0, p)
    lax.fori_loop(0, TICKS, tick, 0)

    @pl.when(c == xe)
    def _():
        def sent(j, carry):
            for core in (0, 1):
                @pl.when((j > 0) | (core != c))
                def _():
                    gap_copy(0, j, core).wait_send()

                gap_copy(1, j, core).wait_send()
            return carry

        lax.fori_loop(0, STEPS, sent, 0)

    rows = STEPS * 128
    stores = [
        pltpu.make_async_copy(src, dst, out_s.at[k])
        for k, (src, dst) in enumerate(((gu, gu_hbm), (gd, gd_hbm), (gr, gr_hbm), (gi, gi_hbm)))
    ]
    for k, (source, values, out) in enumerate(((ax, inn, gu), (ad, wgt, gd))):
        out[...] = dot(source[...].reshape(rows, 384), values[...].reshape(rows, 1024), (0, 0)).astype(BF16)
        stores[k].start()

    gather_wait(32, along_expert, lambda i: dd, ddr, dd_s, dd_r)

    def add_router(k, acc):
        for u in (0, 1):
            d = chip_of(u, k)
            for core in (0, 1):
                meta = tb[u, k, core, 64:80, 0:64].astype(F32)
                grad = signed_hot(meta[0:1], meta[8:9]) * jnp.broadcast_to(ddr[2 * d + core][:, 0:64], (16, 64))
                acc = acc + dot2(grad, tb[u, k, core, 0:64], (1, 0))
        return acc

    gr[...] = lax.fori_loop(0, STEPS, add_router, jnp.zeros((16, 384), F32))[0:4]
    stores[2].start()

    def returned(j, carry):
        @pl.when(j > 0)
        def _():
            cp = ret_copy(0, j)
            cp.wait_send()
            cp.wait_recv()

        cp = ret_copy(1, j)
        cp.wait_send()
        cp.wait_recv()
        return carry

    lax.fori_loop(0, STEPS, returned, 0)
    sums = []
    for e in range(4):
        acc = ret[4 * e].astype(F32)
        for k in range(1, 4):
            acc = acc + ret[4 * e + k].astype(F32)
        sums.append(acc)
    high, low = split(jnp.concatenate(sums, axis=0))
    pick = ph[...]
    value = tb[0, 0, c, 80:144].astype(F32) + (dot(pick, high, (0, 0)) + dot(pick, low, (0, 0)))
    high, low = split(signed_hot(a_own, b_own) * jnp.broadcast_to(dd[:, 0:64], (16, 64)))
    weight = rw[...]
    value = value + (dot(high, weight, (0, 0)) + dot(low, weight, (0, 0)))
    gi[...] = value.astype(BF16)
    stores[3].start()
    for store in stores:
        store.wait()


def place(*refs):
    sources, outs, held, (arrive, leave) = refs[:4], refs[4:8], refs[8:12], refs[12:]
    pieces = [(1, 0, 192), (1, 192, 192), (2, 0, 192), (2, 192, 192), (0, 0, 64), (3, 0, 4)]
    loads, stores = [], []
    for n, (k, low, size) in enumerate(pieces):
        rows = pl.ds(low, size)
        loads.append(pltpu.make_async_copy(sources[k].at[rows], held[k].at[rows], arrive.at[n]))
        stores.append(pltpu.make_async_copy(held[k].at[rows], outs[k].at[rows], leave.at[n]))
    for load in loads:
        load.start()
    for load, store in zip(loads, stores):
        load.wait()
        store.start()
    for store in stores:
        store.wait()


def local(inputs, grad_out, expert_ids, live_counts, router_weight, up_weight, down_weight):
    vmem = pl.BlockSpec(memory_space=pltpu.VMEM)
    dma = pltpu.SemaphoreType.DMA
    anywhere = pl.BlockSpec(memory_space=pl.ANY)
    grads = jax.ShapeDtypeStruct((384, 1024), BF16)
    shapes = (jax.ShapeDtypeStruct((64, 384), BF16), grads, grads, jax.ShapeDtypeStruct((4, 384), F32))
    results = pl.pallas_call(
        kernel,
        out_shape=shapes,
        in_specs=[anywhere, anywhere, vmem, pl.BlockSpec(memory_space=pltpu.SMEM), vmem, anywhere, anywhere],
        out_specs=(anywhere,) * 4,
        scratch_shapes=[
            pltpu.VMEM((384, 1024), BF16),
            pltpu.VMEM((384, 1024), BF16),
            pltpu.VMEM((16, 384), BF16),
            pltpu.VMEM((64, 384), BF16),
            pltpu.VMEM((384, 1024), BF16),
            pltpu.VMEM((384, 1024), BF16),
            pltpu.VMEM((4, 384), F32),
            pltpu.VMEM((2, STEPS, 2, ROWS, 384), BF16),
            pltpu.VMEM((2, STEPS, 2, 32, 64), BF16),
            pltpu.VMEM((128, 64), BF16),
            pltpu.VMEM((STEPS, 128, 384), BF16),
            pltpu.VMEM((STEPS, 128, 384), BF16),
            pltpu.VMEM((STEPS, 4, 16, 32, 128), BF16),
            pltpu.VMEM((STEPS, 4, 8, 32, 128), BF16),
            pltpu.VMEM((STEPS, 4, 4, 32, 128), BF16),
            pltpu.VMEM((STEPS, 4, 3, 32, 128), BF16),
            pltpu.VMEM((STEPS, 4, 16, 32, 128), BF16),
            pltpu.VMEM((STEPS, 128, 1024), BF16),
            pltpu.VMEM((STEPS, 128, 1024), BF16),
            pltpu.VMEM((STEPS, 2, 64, 384), BF16),
            pltpu.VMEM((STEPS, 64, 384), BF16),
            pltpu.VMEM((STEPS, 64, 384), BF16),
            pltpu.VMEM((16, 32, 384), BF16),
            pltpu.VMEM((8, 128), F32),
            pltpu.VMEM((16, 8, 128), F32),
            pltpu.VMEM((1, 128), F32),
            pltpu.VMEM((32, 1, 128), F32),
            pltpu.VMEM((16, 1, 128), F32),
            pltpu.VMEM((16, 16, 1, 128), F32),
            pltpu.VMEM((32, 1, 128), F32),
            pltpu.VMEM((32, 1, 128), F32),
            pltpu.VMEM((1, 128), F32),
            pltpu.VMEM((32, 1, 128), F32),
            dma((2, 2, STEPS)), dma((2, 2, STEPS)),
            dma((2, 2, STEPS)), dma((2, 2, STEPS)),
            dma((STEPS, 20)), dma((STEPS, 20)),
            dma((STEPS, 20)), dma((STEPS, 20)),
            dma((STEPS,)), dma((STEPS,)),
            dma((2, STEPS)), dma((2, STEPS)),
            dma((16,)), dma((16,)),
            dma((2, STEPS, 2)), dma((2, STEPS)),
            dma((16,)), dma((16,)),
            dma((32,)), dma((32,)),
            dma((32,)), dma((32,)),
            dma((4,)), dma((4,)),
        ],
        compiler_params=pltpu.CompilerParams(
            collective_id=0, has_side_effects=True, vmem_limit_bytes=56 * 2**20
        ),
        name="moe_backward",
    )(inputs, grad_out, expert_ids.T, live_counts, router_weight.T, up_weight, down_weight)
    grad_inputs, grad_up, grad_down, grad_router = pl.pallas_call(
        place,
        out_shape=shapes,
        in_specs=[anywhere] * 4,
        out_specs=(anywhere,) * 4,
        scratch_shapes=[pltpu.VMEM(shape.shape, shape.dtype) for shape in shapes] + [dma((6,)), dma((6,))],
        name="place",
    )(*results)
    return grad_inputs, grad_up, grad_down, grad_router.T


def solution(mesh):
    placed = (
        P("expert", "dp"),
        P("expert", "dp"),
        P("expert", None),
        P("expert"),
        P("dp", None),
        P("dp", "expert"),
        P("dp", "expert"),
    )
    return jax.shard_map(
        local,
        mesh=mesh,
        in_specs=placed,
        out_specs=(P("expert", "dp"), P("dp", "expert"), P("dp", "expert"), P("dp", None)),
        check_vma=False,
    )
```

```python
import jax
import jax.numpy as jnp
from jax import lax
from jax.experimental import pallas as pl
from jax.experimental.pallas import tpu as pltpu
from jax.sharding import PartitionSpec as P

MESH = pl.DeviceIdType.MESH
F32 = jnp.float32
BF16 = jnp.bfloat16
ROOT_HALF = 0.7071067811865476
INV_ROOT_TWO_PI = 0.3989422804014327

ORDERS = ((0, 2, 1, 3), (2, 1, 3, 0), (1, 3, 0, 2), (3, 0, 2, 1))
STEPS = 8
TICKS = 15
ROWS = 144
PARTS = ((0, 80), (80, 64))


def split(value):
    high = value.astype(BF16)
    return high, (value - high.astype(F32)).astype(BF16)


def dot(a, b, contract):
    return lax.dot_general(a, b, ((contract[:1], contract[1:]), ((), ())), preferred_element_type=F32)


def dot2(a, b, contract):
    high, low = split(a)
    return dot(high, b, contract) + dot(low, b, contract)


def route(pairs):
    row = lax.broadcasted_iota(jnp.int32, (16, 64), 0)
    hits = [jnp.where((a == e) | (b == e), 1.0, 0.0) for a, b, e in pairs]
    table = jnp.zeros((16, 64), F32)
    for k, hit in enumerate(hits):
        table = jnp.where(row == k, jnp.broadcast_to(hit, (16, 64)), table)
    upper = lax.broadcasted_iota(jnp.int32, (64, 64), 0) < lax.broadcasted_iota(jnp.int32, (64, 64), 1)
    rank = dot(table.astype(BF16), jnp.where(upper, 1.0, 0.0).astype(BF16), (1, 0))
    slot = lax.broadcasted_iota(jnp.int32, (32, 64), 0).astype(F32)
    picks = []
    for k, hit in enumerate(hits):
        at = jnp.broadcast_to(rank[k : k + 1], (32, 64))
        picks.append(jnp.where(slot == at, jnp.broadcast_to(hit, (32, 64)), 0.0).astype(BF16))
    return picks


def signed_hot(a_row, b_row):
    row = lax.broadcasted_iota(jnp.int32, (16, 64), 0).astype(F32)
    first = jnp.where(row == jnp.broadcast_to(a_row, (16, 64)), 1.0, 0.0)
    second = jnp.where(row == jnp.broadcast_to(b_row, (16, 64)), 1.0, 0.0)
    return first - second


def kernel(
    x_hbm, d_hbm, ids_ref, live_ref, rwt_ref, up_hbm, down_hbm,
    gi_hbm, gu_hbm, gd_hbm, gr_hbm,
    up_ref, down_ref, rw, gi, gu, gd, gr, tb, pb, ph, ax, ad, part, rs0, rs1, rs2, ag, inn, wgt, pi, sx, rb, ret,
    ls, lr, gap, gaps, gp, gpr, gs, gret, dd, ddr,
    z_s, z_r, b_s, b_r, rs_s, rs_r, ag_s, ag_r, sx_s, sx_r, ret_s, ret_r,
    l_s, l_r, gap_s, gap_r, gp_s, gp_r, gr_s, gr_r, dd_s, dd_r, in_s, out_s,
):
    dp = lax.axis_index("dp")
    ex = lax.axis_index("expert")
    x, y = lax.rem(dp, 4), dp // 4
    z, c = ex // 2, lax.rem(ex, 2)
    expert = (z // 4).astype(F32)
    xe, ye = lax.rem((x + 1) // 2, 2), lax.rem((y + 1) // 2, 2)
    bits = (xe, x // 2, ye, y // 2)

    def partner(dims):
        px, py = x, y
        if 0 in dims:
            px = x + 1 - 2 * lax.rem(x, 2)
        if 1 in dims:
            px = 3 - x
        if 2 in dims:
            py = y + 1 - 2 * lax.rem(y, 2)
        if 3 in dims:
            py = 3 - y
        return (py * 4 + px, ex)

    sibling = (dp, z * 2 + 1 - c)
    above = (dp, lax.rem(z + 1, 16) * 2 + c)
    below = (dp, lax.rem(z + 15, 16) * 2 + c)

    def copy(src, dst, send, recv, device):
        return pltpu.make_async_remote_copy(
            src_ref=src, dst_ref=dst, send_sem=send, recv_sem=recv, device_id=device, device_id_type=MESH
        )

    def along_expert(i):
        return (dp, lax.rem(ex + i, 32)), lax.rem(ex + 32 - i, 32)

    def along_dp(i):
        return (lax.rem(dp + i, 16), ex), lax.rem(dp + 16 - i, 16)

    def spread(n, peer, source, table, mine, send, recv):
        def one(i, carry):
            device, _ = peer(i)
            copy(source(i), table.at[mine], send.at[i], recv.at[i], device).start()
            return carry

        lax.fori_loop(1, n, one, 0)

    def gather_wait(n, peer, source, table, send, recv):
        def one(i, carry):
            device, origin = peer(i)
            c = copy(source(i), table.at[origin], send.at[i], recv.at[i], device)
            c.wait_send()
            c.wait_recv()
            return carry

        lax.fori_loop(1, n, one, 0)

    loads = [
        pltpu.make_async_copy(src, dst, in_s.at[k])
        for k, (src, dst) in enumerate(
            (
                (x_hbm, tb.at[0, 0, c, pl.ds(0, 64)]),
                (d_hbm, tb.at[0, 0, c, pl.ds(80, 64)]),
                (up_hbm, up_ref),
                (down_hbm, down_ref),
            )
        )
    ]
    for load in loads:
        load.start()
    barrier = pltpu.get_barrier_semaphore()

    def greet_dp(i, carry):
        pl.semaphore_signal(barrier, inc=1, device_id=along_dp(i)[0], device_id_type=MESH)
        return carry

    for device in (above, below, sibling):
        pl.semaphore_signal(barrier, inc=1, device_id=device, device_id_type=MESH)
    lax.fori_loop(1, 16, greet_dp, 0)

    ids = ids_ref[...].astype(F32)
    alive = lax.broadcasted_iota(jnp.int32, (1, 64), 1) < live_ref[0]
    a_own = jnp.where(alive, ids[0:1], -1.0)
    b_own = jnp.where(alive, ids[1:2], -1.0)
    tb[0, 0, c, 64:80] = jnp.zeros((16, 384), BF16)
    low_half = lax.broadcasted_iota(jnp.int32, (16, 64), 0) < 8
    both = jnp.where(low_half, jnp.broadcast_to(a_own, (16, 64)), jnp.broadcast_to(b_own, (16, 64)))
    tb[0, 0, c, 64:80, 0:64] = both.astype(BF16)
    rw[...] = jnp.zeros_like(rw)
    rw[0:4] = rwt_ref[...]
    ls[...] = jnp.zeros_like(ls)
    for load in loads[0:2]:
        load.wait()
    ls[:, 0:64] = dot(rw[...], tb[0, 0, c, 0:64], (1, 1))[0:8]
    gp[...] = jnp.zeros_like(gp)
    gap[...] = jnp.zeros_like(gap)
    dd[...] = jnp.zeros_like(dd)

    pl.semaphore_wait(barrier, 18)

    def z_copy(p, u, src, dst):
        low, size = PARTS[p]
        rows = pl.ds(low, size)
        return copy(
            tb.at[u if src is not None else 0, src if src is not None else 0, c, rows],
            tb.at[u, dst, c, rows],
            z_s.at[p, u, dst],
            z_r.at[p, u, dst],
            above if u == 0 else below,
        )

    def b_copy(p, u, j, core):
        low, size = PARTS[p]
        rows = pl.ds(low, size)
        return copy(tb.at[u, j, core, rows], tb.at[u, j, core, rows], b_s.at[p, u, j], b_r.at[p, u, j], sibling)

    for p in (0, 1):
        z_copy(p, 0, None, 1).start()
        z_copy(p, 1, None, 0).start()
        b_copy(p, 0, 0, c).start()
    spread(16, along_dp, lambda i: ls, lr, dp, l_s, l_r)
    lr[dp] = ls[...]
    for e, pick in enumerate(route([(a_own, b_own, float(e)) for e in range(4)])):
        ph[e * 32 : e * 32 + 32, :] = pick

    def z_step(t, p):
        @pl.when(t < STEPS - 1)
        def _():
            z_copy(p, 0, t, t + 1).wait_recv()

            @pl.when(t < STEPS - 2)
            def _():
                z_copy(p, 0, t + 1, t + 2).start()

            b_copy(p, 0, t + 1, c).start()

        @pl.when(t < STEPS)
        def _():
            z_copy(p, 1, t, t).wait_recv()

            @pl.when(t < STEPS - 1)
            def _():
                z_copy(p, 1, t, t + 1).start()

            b_copy(p, 1, t, c).start()

    def z_sent(t, p):
        @pl.when((t > 0) & (t < STEPS))
        def _():
            z_copy(p, 0, t - 1, t).wait_send()

        @pl.when((t > 0) & (t < STEPS + 1))
        def _():
            z_copy(p, 1, t - 1, t - 1).wait_send()

    def info(q):
        order = ORDERS[q]
        return order, tuple(bits[d] for d in order)

    def rs_sem(which, j, q, m):
        return which.at[j, q * 5 + m]

    def rs_copy(j, q, m):
        order, b = info(q)
        if m == 0:
            src, dst = part.at[j, q, pl.ds((1 - b[0]) * 8, 8)], rs0.at[j, q]
            dims = order[:1]
        elif m == 1:
            src, dst = part.at[j, q, pl.ds(b[0] * 8 + (1 - b[1]) * 4, 4)], rs1.at[j, q]
            dims = order[1:2]
        else:
            mask = m - 1
            src = part.at[j, q, pl.ds(b[0] * 8 + b[1] * 4 + local(b, mask), 1)]
            dst = rs2.at[j, q, pl.ds(mask - 1, 1)]
            dims = tuple(d for k, d in enumerate(order[2:]) if mask & (2 >> k))
        return copy(src, dst, rs_sem(rs_s, j, q, m), rs_sem(rs_r, j, q, m), partner(dims))

    def local(b, mask):
        high = 1 - b[2] if mask & 2 else b[2]
        low = 1 - b[3] if mask & 1 else b[3]
        return high * 2 + low

    def ag_copy(j, q, m, arriving=False):
        order, b = info(q)
        if m == 0:
            dims, size = order[:1], 8
            start = ((1 - b[0]) if arriving else b[0]) * 8
        elif m == 1:
            dims, size = order[1:2], 4
            start = b[0] * 8 + ((1 - b[1]) if arriving else b[1]) * 4
        else:
            mask = m - 1
            dims, size = tuple(d for k, d in enumerate(order[2:]) if mask & (2 >> k)), 1
            start = b[0] * 8 + b[1] * 4 + local(b, mask if arriving else 0)
        ref = ag.at[j, q, pl.ds(start, size)]
        return copy(ref, ref, rs_sem(ag_s, j, q, m), rs_sem(ag_r, j, q, m), partner(dims))

    def start_units(j):
        keys = [(u, core) for core in (0, 1) for u in (0, 1)]
        for u in (0, 1):
            wait_sibling(u, j)
        pairs = []
        for u, core in keys:
            meta = tb[u, j, core, 64:80, 0:64].astype(F32)
            pairs.append((meta[0:1], meta[8:9], expert))
        picks = route(pairs)
        for (u, core), pick in zip(keys, picks):
            pb[u, j, core] = pick
        for a, (low, weight, keep) in enumerate(((0, up_ref, ax), (80, down_ref, ad))):
            rows = [
                dot(pick, tb[u, j, core, low : low + 64], (1, 0)).astype(BF16)
                for (u, core), pick in zip(keys, picks)
            ]
            rows = jnp.concatenate(rows, axis=0)
            keep[j] = rows
            value = dot(rows, weight[...], (1, 0)).astype(BF16)
            for u in (0, 1):
                q = 2 * u + a
                for block in range(16):
                    bit = (block >> 3 & 1, block >> 2 & 1, block >> 1 & 1, block & 1)
                    spot = sum(bit[d] << (3 - k) for k, d in enumerate(ORDERS[q]))
                    row, column = bit[0] * 64 + u * 32, (bit[1] * 4 + bit[2] * 2 + bit[3]) * 128
                    part[j, q, spot] = value[row : row + 32, column : column + 128]
                rs_copy(j, q, 0).start()

    def wait_sibling(u, j):
        for p in (0, 1):
            cp = b_copy(p, u, j, 1 - c)
            cp.wait_send()
            cp.wait_recv()

    def reduce_one(j):
        for q in range(4):
            _, b = info(q)
            rs_copy(j, q, 0).wait_recv()
            near = (1 - b[1]) * 4
            part[j, q, pl.ds(b[0] * 8 + near, 4)] += rs0[j, q, pl.ds(near, 4)]
            rs_copy(j, q, 1).start()
            near = b[1] * 4
            part[j, q, pl.ds(b[0] * 8 + near, 4)] += rs0[j, q, pl.ds(near, 4)]
            rs_copy(j, q, 0).wait_send()

    def reduce_two(j):
        for q in range(4):
            _, b = info(q)
            rs_copy(j, q, 1).wait_recv()
            for mask in (3, 1, 2, 0):
                at = local(b, mask)
                part[j, q, b[0] * 8 + b[1] * 4 + at] += rs1[j, q, at]
                if mask:
                    rs_copy(j, q, mask + 1).start()
            rs_copy(j, q, 1).wait_send()

    def chip_of(u, j):
        return lax.rem(z + 16 - j, 16) if u == 0 else lax.rem(z + j + 1, 16)

    def total(j, q):
        _, b = info(q)
        parts = rs2[j, q].astype(F32)
        own = part[j, q, b[0] * 8 + b[1] * 4 + b[2] * 2 + b[3]].astype(F32)
        return own + parts[0] + parts[1] + parts[2]

    def gap_copy(u, j, core):
        target = lax.rem(z + j, 16) if u == 0 else lax.rem(z + 15 - j, 16)
        return copy(gap, gaps.at[ex], gap_s.at[u, j, core], gap_r.at[u, j], (dp, target * 2 + core))

    def gap_wait(u, j):
        origin = chip_of(u, j) * 2 + xe
        copy(gap, gaps.at[origin], gap_s.at[u, j, 0], gap_r.at[u, j], sibling).wait_recv()

    def activate(j):
        @pl.when((j > 0) | (c != xe))
        def _():
            gap_wait(0, j)

        gap_wait(1, j)
        for q in range(4):
            for mask in (1, 2, 3):
                rs_copy(j, q, mask + 1).wait_recv()
        before = jnp.concatenate([total(j, 0), total(j, 2)], axis=0)
        back = jnp.concatenate([total(j, 1), total(j, 3)], axis=0)
        gates = []
        for u in (0, 1):
            meta = tb[u, j, xe, 64:80, 0:64].astype(F32)
            gap_row = gaps[2 * chip_of(u, j) + xe][:, 0:64]
            gate_row = jnp.where(
                meta[0:1] == expert,
                jax.nn.sigmoid(gap_row),
                jnp.where(meta[8:9] == expert, jax.nn.sigmoid(-gap_row), 0.0),
            )
            gate_row = gate_row.astype(BF16).astype(F32)
            gates.append(
                jnp.sum(pb[u, j, xe].astype(F32) * jnp.broadcast_to(gate_row, (32, 64)), axis=1, keepdims=True)
            )
        gate = jnp.concatenate(gates, axis=0)
        bell = 0.5 * (1.0 + lax.erf(before * ROOT_HALF))
        active = before * bell
        slope = bell + before * jnp.exp(-0.5 * before * before) * INV_ROOT_TWO_PI
        inner = (gate * back * slope).astype(BF16)
        weighted = (gate * active).astype(BF16)
        product = active.astype(BF16).astype(F32) * back
        high, low = split(product)
        ones = jnp.ones((16, 128), BF16)
        sums = dot(ones, high, (1, 1)) + dot(ones, low, (1, 1))
        for q in range(4):
            _, b = info(q)
            u, tile = q // 2, (inner, weighted)[q % 2]
            ag[j, q, b[0] * 8 + b[1] * 4 + b[2] * 2 + b[3]] = tile[u * 32 : u * 32 + 32]
        for q in range(4):
            for mask in (3, 1, 2):
                ag_copy(j, q, mask + 1).start()
        for u in (0, 1):
            gp[chip_of(u, j), :, 0:32] = sums[0:1, u * 32 : u * 32 + 32]
        for q in range(4):
            for mask in (1, 2, 3):
                rs_copy(j, q, mask + 1).wait_send()

    def gather_one(j):
        for q in range(4):
            for mask in (1, 2, 3):
                ag_copy(j, q, mask + 1, True).wait_recv()
            ag_copy(j, q, 1).start()
            for mask in (1, 2, 3):
                ag_copy(j, q, mask + 1).wait_send()

    def gather_two(j):
        for q in range(4):
            ag_copy(j, q, 1, True).wait_recv()
            ag_copy(j, q, 0).start()
            ag_copy(j, q, 1).wait_send()

    def sx_copy(j):
        return copy(pi.at[j, 1 - c], sx.at[j], sx_s.at[j], sx_r.at[j], sibling)

    def finish_unit(j):
        for q in range(4):
            ag_copy(j, q, 0, True).wait_recv()
            ag_copy(j, q, 0).wait_send()
            u, into = q // 2, (inn, wgt)[q % 2]
            for block in range(16):
                bit = (block >> 3 & 1, block >> 2 & 1, block >> 1 & 1, block & 1)
                spot = sum(bit[d] << (3 - k) for k, d in enumerate(ORDERS[q]))
                row, column = bit[0] * 64 + u * 32, (bit[1] * 4 + bit[2] * 2 + bit[3]) * 128
                into[j, row : row + 32, column : column + 128] = ag[j, q, spot]
        value = dot(inn[j], up_ref[...], (1, 1)).astype(BF16)
        pi[j, 0] = value[0:64]
        pi[j, 1] = value[64:128]
        sx_copy(j).start()

    def ret_copy(u, j):
        device = (dp, chip_of(u, j) * 2 + c)
        return copy(rb.at[j, pl.ds(u * 32, 32)], ret.at[z], ret_s.at[u, j], ret_r.at[u, j], device)

    def return_unit(j):
        sx_copy(j).wait_recv()
        sx_copy(j).wait_send()
        rb[j] = (pi[j, c].astype(F32) + sx[j].astype(F32)).astype(BF16)

        @pl.when(j == 0)
        def _():
            ret[z] = rb[0, 0:32]

        @pl.when(j > 0)
        def _():
            ret_copy(0, j).start()

        ret_copy(1, j).start()

    def tick(t, carry):
        def stage(lag, action):
            @pl.when((t >= lag) & (t < lag + STEPS))
            def _():
                action(t - lag)

        stage(0, start_units)
        z_step(t + 1, 0)
        z_sent(t + 1, 0)
        z_step(t + 1, 1)
        z_sent(t + 1, 1)
        stage(1, reduce_one)
        stage(2, reduce_two)

        @pl.when(t == 0)
        def _():
            gather_wait(16, along_dp, lambda i: ls, lr, l_s, l_r)
            logits = jnp.sum(lr[...], axis=0)
            hot = signed_hot(a_own, b_own)[0:8]
            gap[:, 0:64] = jnp.sum(logits[:, 0:64] * hot, axis=0, keepdims=True)
            gaps[ex] = gap[...]

        @pl.when((c == xe) & (t < STEPS))
        def _():
            for core in (0, 1):
                @pl.when((t > 0) | (core != c))
                def _():
                    gap_copy(0, t, core).start()

        @pl.when((c == xe) & (t > 0) & (t < STEPS + 1))
        def _():
            for core in (0, 1):
                gap_copy(1, t - 1, core).start()

        stage(3, activate)

        @pl.when(t == 10)
        def _():
            gpr[dp] = gp[...]
            spread(16, along_dp, lambda i: gp, gpr, dp, gp_s, gp_r)

        stage(4, gather_one)
        stage(5, gather_two)
        stage(6, finish_unit)
        stage(7, return_unit)

        @pl.when(t == 11)
        def _():
            gather_wait(16, along_dp, lambda i: gp, gpr, gp_s, gp_r)
            for half in (0, 1):
                mine = [k for k in range(16) if ((k % 4 + 1) // 2) % 2 == half]
                acc = gpr[mine[0]]
                for k in mine[1:]:
                    acc = acc + gpr[k]
                for k in range(16):
                    gs[2 * k + half] = acc[k].astype(BF16).astype(F32)
            gret[ex] = gs[ex]
            spread(32, along_expert, lambda i: gs.at[along_expert(i)[0][1]], gret, ex, gr_s, gr_r)

        @pl.when(t == 13)
        def _():
            gather_wait(32, along_expert, lambda i: gs.at[along_expert(i)[0][1]], gret, gr_s, gr_r)
            picked = []
            for e in range(4):
                row = gret[8 * e]
                for k in range(1, 8):
                    row = row + gret[8 * e + k]
                row = jnp.broadcast_to(row[:, 0:32], (16, 32))
                picked.append(dot2(row, ph[e * 32 : e * 32 + 32, :], (1, 0))[0:1])
            first = jnp.zeros((1, 64), F32)
            second = jnp.zeros((1, 64), F32)
            for e in range(4):
                first = first + jnp.where(a_own == float(e), picked[e], 0.0)
                second = second + jnp.where(b_own == float(e), picked[e], 0.0)
            row = gap[:, 0:64]
            gate0 = jax.nn.sigmoid(row).astype(BF16).astype(F32)
            gate1 = jax.nn.sigmoid(-row).astype(BF16).astype(F32)
            delta0 = (first * gate0 * (1.0 - gate0)).astype(BF16).astype(F32)
            delta1 = (second * gate1 * (1.0 - gate1)).astype(BF16).astype(F32)
            dd[:, 0:64] = delta0 - delta1
            ddr[ex] = dd[...]
            spread(32, along_expert, lambda i: dd, ddr, ex, dd_s, dd_r)

        return carry

    for load in loads[2:]:
        load.wait()
    for p in (0, 1):
        z_step(0, p)
    lax.fori_loop(0, TICKS, tick, 0)

    @pl.when(c == xe)
    def _():
        def sent(j, carry):
            for core in (0, 1):
                @pl.when((j > 0) | (core != c))
                def _():
                    gap_copy(0, j, core).wait_send()

                gap_copy(1, j, core).wait_send()
            return carry

        lax.fori_loop(0, STEPS, sent, 0)

    rows = STEPS * 128
    stores = [
        pltpu.make_async_copy(src, dst, out_s.at[k])
        for k, (src, dst) in enumerate(((gu, gu_hbm), (gd, gd_hbm), (gr, gr_hbm), (gi, gi_hbm)))
    ]
    for k, (source, values, out) in enumerate(((ax, inn, gu), (ad, wgt, gd))):
        out[...] = dot(source[...].reshape(rows, 384), values[...].reshape(rows, 1024), (0, 0)).astype(BF16)
        stores[k].start()

    gather_wait(32, along_expert, lambda i: dd, ddr, dd_s, dd_r)

    def add_router(k, acc):
        for u in (0, 1):
            d = chip_of(u, k)
            for core in (0, 1):
                meta = tb[u, k, core, 64:80, 0:64].astype(F32)
                grad = signed_hot(meta[0:1], meta[8:9]) * jnp.broadcast_to(ddr[2 * d + core][:, 0:64], (16, 64))
                acc = acc + dot2(grad, tb[u, k, core, 0:64], (1, 0))
        return acc

    gr[...] = lax.fori_loop(0, STEPS, add_router, jnp.zeros((16, 384), F32))[0:4]
    stores[2].start()

    def returned(j, carry):
        @pl.when(j > 0)
        def _():
            cp = ret_copy(0, j)
            cp.wait_send()
            cp.wait_recv()

        cp = ret_copy(1, j)
        cp.wait_send()
        cp.wait_recv()
        return carry

    lax.fori_loop(0, STEPS, returned, 0)
    sums = []
    for e in range(4):
        acc = ret[4 * e].astype(F32)
        for k in range(1, 4):
            acc = acc + ret[4 * e + k].astype(F32)
        sums.append(acc)
    high, low = split(jnp.concatenate(sums, axis=0))
    pick = ph[...]
    value = tb[0, 0, c, 80:144].astype(F32) + (dot(pick, high, (0, 0)) + dot(pick, low, (0, 0)))
    high, low = split(signed_hot(a_own, b_own) * jnp.broadcast_to(dd[:, 0:64], (16, 64)))
    weight = rw[...]
    value = value + (dot(high, weight, (0, 0)) + dot(low, weight, (0, 0)))
    gi[...] = value.astype(BF16)
    stores[3].start()
    for store in stores:
        store.wait()


def place(*refs):
    sources, outs, held, (arrive, leave) = refs[:4], refs[4:8], refs[8:12], refs[12:]
    pieces = [(1, 0, 192), (1, 192, 192), (2, 0, 192), (2, 192, 192), (0, 0, 64), (3, 0, 4)]
    loads, stores = [], []
    for n, (k, low, size) in enumerate(pieces):
        rows = pl.ds(low, size)
        loads.append(pltpu.make_async_copy(sources[k].at[rows], held[k].at[rows], arrive.at[n]))
        stores.append(pltpu.make_async_copy(held[k].at[rows], outs[k].at[rows], leave.at[n]))
    for load in loads:
        load.start()
    for load, store in zip(loads, stores):
        load.wait()
        store.start()
    for store in stores:
        store.wait()


def local(inputs, grad_out, expert_ids, live_counts, router_weight, up_weight, down_weight):
    vmem = pl.BlockSpec(memory_space=pltpu.VMEM)
    dma = pltpu.SemaphoreType.DMA
    anywhere = pl.BlockSpec(memory_space=pl.ANY)
    grads = jax.ShapeDtypeStruct((384, 1024), BF16)
    shapes = (jax.ShapeDtypeStruct((64, 384), BF16), grads, grads, jax.ShapeDtypeStruct((4, 384), F32))
    results = pl.pallas_call(
        kernel,
        out_shape=shapes,
        in_specs=[anywhere, anywhere, vmem, pl.BlockSpec(memory_space=pltpu.SMEM), vmem, anywhere, anywhere],
        out_specs=(anywhere,) * 4,
        scratch_shapes=[
            pltpu.VMEM((384, 1024), BF16),
            pltpu.VMEM((384, 1024), BF16),
            pltpu.VMEM((16, 384), BF16),
            pltpu.VMEM((64, 384), BF16),
            pltpu.VMEM((384, 1024), BF16),
            pltpu.VMEM((384, 1024), BF16),
            pltpu.VMEM((4, 384), F32),
            pltpu.VMEM((2, STEPS, 2, ROWS, 384), BF16),
            pltpu.VMEM((2, STEPS, 2, 32, 64), BF16),
            pltpu.VMEM((128, 64), BF16),
            pltpu.VMEM((STEPS, 128, 384), BF16),
            pltpu.VMEM((STEPS, 128, 384), BF16),
            pltpu.VMEM((STEPS, 4, 16, 32, 128), BF16),
            pltpu.VMEM((STEPS, 4, 8, 32, 128), BF16),
            pltpu.VMEM((STEPS, 4, 4, 32, 128), BF16),
            pltpu.VMEM((STEPS, 4, 3, 32, 128), BF16),
            pltpu.VMEM((STEPS, 4, 16, 32, 128), BF16),
            pltpu.VMEM((STEPS, 128, 1024), BF16),
            pltpu.VMEM((STEPS, 128, 1024), BF16),
            pltpu.VMEM((STEPS, 2, 64, 384), BF16),
            pltpu.VMEM((STEPS, 64, 384), BF16),
            pltpu.VMEM((STEPS, 64, 384), BF16),
            pltpu.VMEM((16, 32, 384), BF16),
            pltpu.VMEM((8, 128), F32),
            pltpu.VMEM((16, 8, 128), F32),
            pltpu.VMEM((1, 128), F32),
            pltpu.VMEM((32, 1, 128), F32),
            pltpu.VMEM((16, 1, 128), F32),
            pltpu.VMEM((16, 16, 1, 128), F32),
            pltpu.VMEM((32, 1, 128), F32),
            pltpu.VMEM((32, 1, 128), F32),
            pltpu.VMEM((1, 128), F32),
            pltpu.VMEM((32, 1, 128), F32),
            dma((2, 2, STEPS)), dma((2, 2, STEPS)),
            dma((2, 2, STEPS)), dma((2, 2, STEPS)),
            dma((STEPS, 20)), dma((STEPS, 20)),
            dma((STEPS, 20)), dma((STEPS, 20)),
            dma((STEPS,)), dma((STEPS,)),
            dma((2, STEPS)), dma((2, STEPS)),
            dma((16,)), dma((16,)),
            dma((2, STEPS, 2)), dma((2, STEPS)),
            dma((16,)), dma((16,)),
            dma((32,)), dma((32,)),
            dma((32,)), dma((32,)),
            dma((4,)), dma((4,)),
        ],
        compiler_params=pltpu.CompilerParams(
            collective_id=0, has_side_effects=True, vmem_limit_bytes=56 * 2**20
        ),
        name="moe_backward",
    )(inputs, grad_out, expert_ids.T, live_counts, router_weight.T, up_weight, down_weight)
    grad_inputs, grad_up, grad_down, grad_router = pl.pallas_call(
        place,
        out_shape=shapes,
        in_specs=[anywhere] * 4,
        out_specs=(anywhere,) * 4,
        scratch_shapes=[pltpu.VMEM(shape.shape, shape.dtype) for shape in shapes] + [dma((6,)), dma((6,))],
        name="place",
    )(*results)
    return grad_inputs, grad_up, grad_down, grad_router.T


def solution(mesh):
    placed = (
        P("expert", "dp"),
        P("expert", "dp"),
        P("expert", None),
        P("expert"),
        P("dp", None),
        P("dp", "expert"),
        P("dp", "expert"),
    )
    return jax.shard_map(
        local,
        mesh=mesh,
        in_specs=placed,
        out_specs=(P("expert", "dp"), P("dp", "expert"), P("dp", "expert"), P("dp", None)),
        check_vma=False,
    )
```
